32 devices in a mesh: group: 2 (over y), batch: 8 (over z, x), tensor: 2 (over core).
Axes of the slice: x: 2, y: 2, z: 4, core: 2. Of those that a mesh axis runs over, the one named last changes fastest.
Arguments:
- features: bfloat16 [32, 8192], P(('group', 'batch'), 'tensor'), parts along dimension 0, may hold values from -6 to 6
- up_weight: bfloat16 [8192, 32768], P('tensor', 'batch'), may hold values from -0.0625 to 0.0625
- adapter_down_weight: bfloat16 [64, 8192, 16], P(('group', 'batch'), 'tensor'), parts along dimension 0, may hold values from -0.0625 to 0.0625
- adapter_up_weight: bfloat16 [64, 16, 32768], P(('group', 'batch'), 'tensor'), parts along dimension 0, may hold values from -1.5 to 1.5
- request_adapter: int32 [32], P('group'), parts along dimension 0, may hold values from 0 to 31, as said below
- adapter_storage_row: int32 [64], P('group'), parts along dimension 0, may hold values from 0 to 31, as said below
Outputs:
- hidden: bfloat16 [32, 32768], P('group', ('batch', 'tensor')), parts along dimension 0
The draws below stay inside these ranges and needn't reach their ends.
There are 2 independent parts, one for each index of `group`. The reference program is written for one: setup_inputs(seed, part) draws one part's arguments, and reference() takes and returns one part's arrays. A program takes and returns all parts, laid end to end along the dimension named above; an argument that names none is the same for every part. Nothing has to cross between parts.
Inputs may be any that keep to these rules, and one draw needn't show every extreme that they name: `request_adapter`: the requests whose adapters have storage rows in [o * 4, (o + 1) * 4) number at most 8 for every o, and exactly 8 for one o. A permutation: adapter a is stored in row adapter_storage_row[a] of adapter_down_weight and adapter_up_weight.
All inputs are finite; a program needn't handle non-finite values.
Results may differ from the reference program's by a relative error of at most 0.0049.
Values may be sent and summed in bfloat16 or wider, within the bound.
No kernel may reach another device: no remote copies, remote signals or barrier semaphores. Data moves between devices by JAX's collectives and lax.ppermute only.
A program may use at most 128 MiB of HBM per device.

```python
import jax
import jax.numpy as jnp
from jax import lax

MODEL_WIDTH = 8192
HIDDEN_UNITS = 32768
ADAPTER_RANK = 16
ADAPT_DEV = 4
BATCH_REQUESTS = 2
ADAPTER_COUNT = 32
REQUEST_COUNT = 16
OWN_MOST = 8


def joint_tables(key):
    key_slot, key_hot, key_order, key_pick = jax.random.split(key, 4)
    slot_table = jax.random.permutation(key_slot, ADAPTER_COUNT).astype(jnp.int32)
    batches = REQUEST_COUNT // BATCH_REQUESTS
    hot_owner = jax.random.randint(key_hot, (), 0, batches).astype(jnp.int32)
    shuffled = jax.random.permutation(key_order, REQUEST_COUNT).astype(jnp.int32)
    position = jnp.arange(REQUEST_COUNT, dtype=jnp.int32)
    others = (hot_owner + 1 + jnp.maximum(position - OWN_MOST, 0) % (batches - 1)) % batches
    owner_at = jnp.where(position < OWN_MOST, hot_owner, others).astype(jnp.int32)
    owner_req = jnp.zeros((REQUEST_COUNT,), jnp.int32).at[shuffled].set(owner_at)
    local_pick = jax.random.randint(key_pick, (REQUEST_COUNT,), 0, ADAPT_DEV).astype(jnp.int32)
    adapter_at = jnp.zeros((ADAPTER_COUNT,), jnp.int32).at[slot_table].set(jnp.arange(ADAPTER_COUNT, dtype=jnp.int32))
    adapter_ids = adapter_at[owner_req * ADAPT_DEV + local_pick]
    return (slot_table, adapter_ids)


def draw_request_adapter(key, part):
    shared = joint_tables(key)
    return shared[1]


def draw_adapter_storage_row(key, part):
    shared = joint_tables(key)
    return shared[0]


def steps_of(key, dims, shards, low, top_value):
    factor_of = 1.0
    for dim, blocks in shards:
        heights = jax.random.uniform(jax.random.fold_in(jax.random.fold_in(key, 6), dim), (blocks,), jnp.float32, low / len(shards), top_value / len(shards))
        factor_of = factor_of * jnp.repeat(jnp.exp(heights), dims[dim] // blocks).reshape((-1,) + (1,) * (len(dims) - 1 - dim))
    return factor_of


def bell_draw(stream_key, extent, width, reach, pieces=(), kind=jnp.bfloat16):
    loudness = steps_of(stream_key, extent, pieces, -0.22, 0.18) if pieces else 1.0
    values = jax.random.normal(stream_key, extent, jnp.float32) * width * loudness
    return jnp.minimum(jnp.maximum(values, -reach), reach).astype(kind)


def setup_inputs(seed: int = 0, part: int = 0) -> dict:
    keys = jax.random.split(jax.random.key(seed), 7)
    part_splits = jax.random.split(jax.random.fold_in(keys[6], part), 7)
    features = bell_draw(part_splits[0], (REQUEST_COUNT, MODEL_WIDTH), 1.0, 6.0, ((0, 8), (1, 2)))
    up_weight = bell_draw(keys[1], (MODEL_WIDTH, HIDDEN_UNITS), MODEL_WIDTH ** -0.5, 0.0625, ((0, 2), (1, 8)))
    adapter_down_weight = bell_draw(part_splits[2], (ADAPTER_COUNT, MODEL_WIDTH, ADAPTER_RANK), MODEL_WIDTH ** -0.5, 0.0625, ((0, 8), (1, 2)))
    adapter_up_weight = bell_draw(part_splits[3], (ADAPTER_COUNT, ADAPTER_RANK, HIDDEN_UNITS), ADAPTER_RANK ** -0.5, 1.5, ((0, 8), (1, 2)))
    request_adapter = draw_request_adapter(jax.random.fold_in(jax.random.fold_in(keys[6], part), 71), part)
    adapter_storage_row = draw_adapter_storage_row(jax.random.fold_in(jax.random.fold_in(keys[6], part), 71), part)
    return dict(features=features, up_weight=up_weight, adapter_down_weight=adapter_down_weight, adapter_up_weight=adapter_up_weight, request_adapter=request_adapter, adapter_storage_row=adapter_storage_row)


def reference(features, up_weight, adapter_down_weight, adapter_up_weight, request_adapter, adapter_storage_row):
    plain_output = jnp.dot(features, up_weight, preferred_element_type=jnp.float32)
    slot_of = adapter_storage_row[request_adapter].astype(jnp.int32)
    block_total = REQUEST_COUNT // BATCH_REQUESTS

    def single_block(inputs):
        block_rows, block_storage_rows = inputs
        down_weight_rows = adapter_down_weight[block_storage_rows].astype(jnp.float32)
        shrunk = jnp.einsum("rd,rdk->rk", block_rows.astype(jnp.float32), down_weight_rows,
                            precision=lax.Precision.HIGHEST).astype(jnp.bfloat16)
        up_weight_rows = adapter_up_weight[block_storage_rows].astype(jnp.float32)
        return jnp.einsum("rk,rkc->rc", shrunk.astype(jnp.float32), up_weight_rows,
                          precision=lax.Precision.HIGHEST)

    adapter_update = lax.map(single_block, (features.reshape(block_total, BATCH_REQUESTS, MODEL_WIDTH),
                                     slot_of.reshape(block_total, BATCH_REQUESTS)))
    adapter_update = adapter_update.reshape(REQUEST_COUNT, HIDDEN_UNITS)
    return jnp.square(jnp.maximum(plain_output + adapter_update, 0.0)).astype(jnp.bfloat16)
```

```python
import functools

import jax
import jax.numpy as jnp
from jax import lax
from jax.experimental import pallas as pl
from jax.experimental.pallas import tpu as pltpu
from jax.sharding import PartitionSpec as P

OWN_MOST = 8
LANES = 128
MIB = 1 << 20
F32 = jnp.float32
BF16 = jnp.bfloat16
VMEM = pltpu.VMEM


def whole(n):
    return [pl.BlockSpec(memory_space=VMEM)] * n


def in_vmem(x):
    return pltpu.with_memory_space_constraint(x, VMEM)


def slots_of(ra, sr):
    requests, adapters = ra.shape[1], sr.shape[1]
    same = lax.broadcasted_iota(jnp.int32, (requests, requests), 0) == lax.broadcasted_iota(
        jnp.int32, (requests, requests), 1
    )
    ra = jnp.sum(jnp.where(same, ra, 0), axis=1, keepdims=True)
    hit = lax.broadcasted_iota(jnp.int32, (requests, adapters), 1) == ra
    return jnp.sum(jnp.where(hit, sr, 0), axis=1, keepdims=True)


def ranks_of(mine):
    requests = mine.shape[0]
    earlier = lax.broadcasted_iota(jnp.int32, (requests, requests), 1) < lax.broadcasted_iota(
        jnp.int32, (requests, requests), 0
    )
    marks = jnp.broadcast_to(mine.astype(F32), (requests, LANES)).astype(BF16)
    return jnp.dot(earlier.astype(F32).astype(BF16), marks, preferred_element_type=F32)[:, :OWN_MOST]


def place_of(slot, owner, adapters_here):
    mine = (slot >= owner * adapters_here) & (slot < (owner + 1) * adapters_here)
    place = lax.broadcasted_iota(jnp.int32, (slot.shape[0], OWN_MOST), 1).astype(F32)
    return jnp.where((ranks_of(mine) == place) & mine, 1.0, 0.0).astype(BF16)


def shrink_kernel(g_ref, down_ref, x_ref, f_ref, rows_ref):
    batches, each, _ = g_ref.shape
    for b in range(batches):
        rows_ref[b * each : (b + 1) * each] = g_ref[b].astype(F32)
    f_ref[...] = rows_ref[...].astype(BF16)
    x_ref[...] = lax.dot_general(
        f_ref[...], down_ref[...], (((1,), (1,)), ((), ())), preferred_element_type=F32
    )


def delta_kernel(adapters_here, ra_ref, sr_ref, x_ref, xo_ref, up_ref, upo_ref, d_ref):
    batches, _, cols = d_ref.shape
    me = lax.axis_index("batch")
    core = lax.axis_index("tensor")
    wide = x_ref.shape[1]
    rank = wide // adapters_here
    half = rank // 2
    slot = slots_of(ra_ref[...], sr_ref[...])
    column = lax.broadcasted_iota(jnp.int32, (slot.shape[0], wide), 1)
    low = (slot - me * adapters_here) * rank
    shrunk = (x_ref[...] + xo_ref[...]).astype(BF16)
    kept = jnp.where((column >= low) & (column < low + rank), shrunk.astype(F32), 0.0).astype(BF16)
    place = place_of(slot, me, adapters_here)
    rows = lax.dot_general(
        place, kept, (((0,), (0,)), ((), ())), preferred_element_type=F32
    ).astype(BF16)
    i = lax.broadcasted_iota(jnp.int32, (wide, wide // 2), 0)
    j = lax.broadcasted_iota(jnp.int32, (wide, wide // 2), 1)
    base = (j // half) * rank + j % half

    def part(c):
        pick = jnp.where(i == base + c * half, 1.0, 0.0).astype(BF16)
        return jnp.dot(rows, pick, preferred_element_type=F32).astype(BF16)

    own, other = part(core), part(1 - core)
    for d in range(batches):
        span = pl.ds(pl.multiple_of((2 * d + core) * cols, LANES), cols)
        total = jnp.dot(own, up_ref[:, span], preferred_element_type=F32)
        total += jnp.dot(other, upo_ref[:, span], preferred_element_type=F32)
        d_ref[d] = total.astype(BF16)


def base_kernel(step, f_ref, w_ref, keep_ref, send_ref):
    core = lax.axis_index("tensor")
    cols = keep_ref.shape[1]
    for k, ref in enumerate((send_ref, keep_ref)):
        first = (core + 1 - k) % 2 * cols
        for t in range(0, cols, step):
            span = pl.ds(pl.multiple_of(first + t, LANES), step)
            ref[:, t : t + step] = jnp.dot(f_ref[...], w_ref[:, span], preferred_element_type=F32)


def final_kernel(adapters_here, ra_ref, sr_ref, keep_ref, got_ref, d_ref, o_ref):
    slot = slots_of(ra_ref[...], sr_ref[...])
    total = keep_ref[...] + got_ref[...]
    for s in range(d_ref.shape[0]):
        total += jnp.dot(place_of(slot, s, adapters_here), d_ref[s], preferred_element_type=F32)
    o_ref[...] = jnp.square(jnp.maximum(total, 0.0)).astype(BF16)


def call(kernel, out, n_in, cost=None, limit=8, scratch=()):
    many = isinstance(out, (list, tuple))
    return pl.pallas_call(
        kernel,
        out_shape=out,
        in_specs=whole(n_in),
        out_specs=whole(len(out)) if many else whole(1)[0],
        compiler_params=pltpu.CompilerParams(vmem_limit_bytes=limit * MIB),
        cost_estimate=cost,
        scratch_shapes=scratch,
    )


def per_device(features, up_weight, down, up, request_adapter, storage_row):
    batches = lax.axis_size("batch")
    adapters_here, width, rank = down.shape
    hidden = up.shape[2]
    requests = request_adapter.shape[0]
    cols = up_weight.shape[1] // 2
    swap = functools.partial(lax.ppermute, axis_name="tensor", perm=[(0, 1), (1, 0)])
    ra = request_adapter.reshape(1, requests)
    sr = storage_row.reshape(1, -1)
    up = up.reshape(-1, hidden)
    up_other = swap(up)
    down = jnp.transpose(down, (0, 2, 1)).reshape(adapters_here * rank, width)
    sent = jnp.broadcast_to(features[None], (batches,) + features.shape)
    gathered = lax.all_to_all(sent, "batch", 0, 0, tiled=True)
    x, rows = call(
        shrink_kernel,
        [
            jax.ShapeDtypeStruct((requests, adapters_here * rank), F32),
            jax.ShapeDtypeStruct((requests, width), BF16),
        ],
        2,
        scratch=[VMEM((requests, width), F32)],
    )(gathered, down)
    x_other = swap(x)
    delta = call(
        functools.partial(delta_kernel, adapters_here),
        jax.ShapeDtypeStruct((batches, OWN_MOST, cols), BF16),
        6,
    )(ra, sr, x, x_other, up, up_other)
    received = lax.all_to_all(delta, "batch", 0, 0, tiled=True)
    half = jax.ShapeDtypeStruct((requests, cols), F32)
    keep, send = call(
        functools.partial(base_kernel, min(cols, 512)),
        [half, half],
        2,
        pl.CostEstimate(
            flops=2 * requests * up_weight.size, bytes_accessed=2 * up_weight.size, transcendentals=0
        ),
    )(rows, in_vmem(up_weight))
    got = swap(send)
    return call(
        functools.partial(final_kernel, adapters_here),
        jax.ShapeDtypeStruct((requests, cols), BF16),
        5,
    )(ra, sr, keep, got, received)


def solution(mesh):
    in_specs = (
        P(("group", "batch"), "tensor"),
        P("tensor", "batch"),
        P(("group", "batch"), "tensor", None),
        P(("group", "batch"), "tensor", None),
        P("group"),
        P("group"),
    )
    return jax.shard_map(
        per_device,
        mesh=mesh,
        in_specs=in_specs,
        out_specs=P("group", ("batch", "tensor")),
        check_vma=False,
    )
```

```python
import functools

import jax
import jax.numpy as jnp
from jax import lax
from jax.experimental import pallas as pl
from jax.experimental.pallas import tpu as pltpu
from jax.sharding import PartitionSpec as P

OWN_MOST = 8
LANES = 128
MIB = 1 << 20
F32 = jnp.float32
BF16 = jnp.bfloat16
VMEM = pltpu.VMEM


def whole(n):
    return [pl.BlockSpec(memory_space=VMEM)] * n


def in_vmem(x):
    return pltpu.with_memory_space_constraint(x, VMEM)


def in_hbm(x):
    return pltpu.with_memory_space_constraint(x, pltpu.HBM)


def copies_kernel(v_ref, o_ref):
    o_ref[...] = jnp.broadcast_to(v_ref[...][None], o_ref.shape)


def ready_kernel(
    batches, ra_ref, sr_ref, down_ref, up_ref, upo_ref, keep_ref, place_ref, sel_ref, downv_ref, upv_ref, sems
):
    me = lax.axis_index("batch")
    core = lax.axis_index("tensor")
    rows, hidden = up_ref.shape
    cols = hidden // (2 * batches)
    copies = [pltpu.make_async_copy(down_ref, downv_ref, sems.at[0])]
    for d in range(batches):
        span = pl.ds(pl.multiple_of((2 * d + core) * cols, LANES), cols)
        for k, ref in enumerate((up_ref, upo_ref)):
            copies.append(
                pltpu.make_async_copy(
                    ref.at[:, span],
                    upv_ref.at[k * rows : (k + 1) * rows, d * cols : (d + 1) * cols],
                    sems.at[1 + 2 * d + k],
                )
            )
    for c in copies:
        c.start()
    requests, adapters = ra_ref.shape[1], sr_ref.shape[1]
    here = adapters // batches

    def iota(shape, dim):
        return lax.broadcasted_iota(jnp.int32, shape, dim)

    square = (requests, requests)
    ra = jnp.sum(jnp.where(iota(square, 0) == iota(square, 1), ra_ref[...], 0), axis=1, keepdims=True)
    slot = jnp.sum(
        jnp.where(iota((requests, adapters), 1) == ra, sr_ref[...], 0), axis=1, keepdims=True
    )
    first = iota((requests, batches), 1) * here
    hit = (slot >= first) & (slot < first + here)
    earlier = jnp.where(iota(square, 1) < iota(square, 0), 1.0, 0.0).astype(BF16)
    marks = jnp.where(hit, 1.0, 0.0)
    counts = jnp.dot(earlier, marks.astype(BF16), preferred_element_type=F32)
    rank = jnp.sum(counts * marks, axis=1, keepdims=True).astype(jnp.int32)
    owner = jnp.sum(jnp.where(hit, iota((requests, batches), 1), 0), axis=1, keepdims=True)
    wide = keep_ref.shape[1]
    width = wide // here
    low = (slot - me * here) * width
    column = iota((requests, wide), 1)
    keep_ref[...] = jnp.where((column >= low) & (column < low + width), 1.0, 0.0)
    mine = (owner == me) & (iota((requests, OWN_MOST), 1) == rank)
    place_ref[...] = jnp.where(mine, 1.0, 0.0).astype(BF16)
    sel_ref[...] = jnp.where(
        iota(sel_ref.shape, 1) == owner * OWN_MOST + rank, 1.0, 0.0
    ).astype(BF16)
    for c in copies:
        c.wait()


def shrink_kernel(g_ref, down_ref, x_ref, f_ref, rows_ref):
    batches, each, _ = g_ref.shape
    for b in range(batches):
        rows_ref[b * each : (b + 1) * each] = g_ref[b].astype(F32)
    f_ref[...] = rows_ref[...].astype(BF16)
    x_ref[...] = lax.dot_general(
        f_ref[...], down_ref[...], (((1,), (1,)), ((), ())), preferred_element_type=F32
    )


def delta_kernel(here, x_ref, xo_ref, keep_ref, place_ref, up_ref, acc_ref, d_ref):
    batches, _, cols = d_ref.shape
    core = lax.axis_index("tensor")
    wide = x_ref.shape[1]
    rank = wide // here
    half = rank // 2
    shrunk = (x_ref[...] + xo_ref[...]).astype(BF16)
    kept = (shrunk.astype(F32) * keep_ref[...]).astype(BF16)
    rows = lax.dot_general(
        place_ref[...], kept, (((0,), (0,)), ((), ())), preferred_element_type=F32
    ).astype(BF16)
    i = lax.broadcasted_iota(jnp.int32, (wide, wide), 0)
    j = lax.broadcasted_iota(jnp.int32, (wide, wide), 1)
    side = jnp.where(j < wide // 2, core, 1 - core)
    k = jnp.where(j < wide // 2, j, j - wide // 2)
    source = jnp.zeros_like(k)
    for h in range(here):
        within = (k >= h * half) & (k < (h + 1) * half)
        source = jnp.where(within, h * rank + k - h * half, source)
    pick = jnp.where(i == source + side * half, 1.0, 0.0).astype(BF16)
    rows = jnp.dot(rows, pick, preferred_element_type=F32).astype(BF16)
    for d in range(batches):
        d_ref[d] = jnp.dot(
            rows, up_ref[:, d * cols : (d + 1) * cols], preferred_element_type=F32
        ).astype(BF16)


def stream(step, first, count, f_ref, w_ref, buf, sems, add):
    depth = buf.shape[0]

    def copy(i):
        return pltpu.make_async_copy(
            w_ref.at[pl.ds((first + i) * step, step)], buf.at[i % depth], sems.at[i % depth]
        )

    for i in range(min(depth, count)):
        copy(i).start()
    for i in range(count):
        copy(i).wait()
        k = (first + i) * step
        add(i, jnp.dot(f_ref[:, k : k + step], buf[i % depth], preferred_element_type=F32))
        if i + depth < count:
            copy(i + depth).start()


def head_kernel(step, count, f_ref, w_ref, acc_ref, buf, sems):
    def add(i, part):
        acc_ref[...] = part if i == 0 else acc_ref[...] + part

    stream(step, 0, count, f_ref, w_ref, buf, sems, add)


def base_kernel(step, first, count, f_ref, head_ref, w_ref, keep_ref, send_ref, acc_ref, buf, sems):
    def add(i, part):
        acc_ref[...] = (head_ref if i == 0 else acc_ref)[...] + part

    stream(step, first, count, f_ref, w_ref, buf, sems, add)
    core = lax.axis_index("tensor")
    cols = keep_ref.shape[1]
    keep_ref[...] = acc_ref[:, pl.ds(pl.multiple_of(core * cols, LANES), cols)]
    send_ref[...] = acc_ref[:, pl.ds(pl.multiple_of((1 - core) * cols, LANES), cols)]


def final_kernel(sel_ref, keep_ref, got_ref, d_ref, o_ref):
    total = keep_ref[...] + got_ref[...]
    total += jnp.dot(sel_ref[...], d_ref[...], preferred_element_type=F32)
    o_ref[...] = jnp.square(jnp.maximum(total, 0.0)).astype(BF16)


def call(kernel, out, places, cost=None, limit=6, scratch=()):
    spec = {"v": pl.BlockSpec(memory_space=VMEM), "h": pl.BlockSpec(memory_space=pltpu.HBM),
            "a": pl.BlockSpec(memory_space=pl.ANY)}
    many = isinstance(out, (list, tuple))
    return pl.pallas_call(
        kernel,
        out_shape=out,
        in_specs=[spec[p] for p in places],
        out_specs=[spec["v"]] * len(out) if many else spec["v"],
        compiler_params=pltpu.CompilerParams(vmem_limit_bytes=limit * MIB),
        cost_estimate=cost,
        scratch_shapes=scratch,
    )


def moves(size, flops=0):
    return pl.CostEstimate(flops=flops, bytes_accessed=size, transcendentals=0)


def per_device(features, up_weight, down, up, request_adapter, storage_row):
    batches = lax.axis_size("batch")
    here, width, rank = down.shape
    hidden = up.shape[2]
    requests = request_adapter.shape[0]
    cols = up_weight.shape[1] // 2
    wide = here * rank
    shape = jax.ShapeDtypeStruct
    dma = pltpu.SemaphoreType.DMA
    swap = functools.partial(lax.ppermute, axis_name="tensor", perm=[(0, 1), (1, 0)])
    up = up.reshape(-1, hidden)
    up_other = swap(up)
    down = jnp.transpose(down, (0, 2, 1)).reshape(wide, width)
    sent = call(copies_kernel, shape((batches,) + features.shape, BF16), "v")(features)
    gathered = lax.all_to_all(sent, "batch", 0, 0, tiled=True)
    keep, place, sel, down, up = call(
        functools.partial(ready_kernel, batches),
        [
            shape((requests, wide), F32),
            shape((requests, OWN_MOST), BF16),
            shape((requests, batches * OWN_MOST), BF16),
            VMEM(down.shape, BF16),
            VMEM((wide, hidden // 2), BF16),
        ],
        "vvhha",
        moves(6 * up.size),
        scratch=[dma((1 + 2 * batches,))],
    )(request_adapter.reshape(1, -1), storage_row.reshape(1, -1), in_hbm(down), in_hbm(up), up_other)
    x, rows = call(
        shrink_kernel,
        [shape((requests, wide), F32), shape((requests, width), BF16)],
        "vv",
        scratch=[VMEM((requests, width), F32)],
    )(gathered, in_vmem(down))
    x_other = swap(x)
    step = 256
    head = 2
    blocks = width // step
    flops = 2 * requests * step * 2 * cols
    acc = call(
        functools.partial(head_kernel, step, head),
        shape((requests, 2 * cols), F32),
        "vh",
        moves(head * 4 * step * cols, head * flops),
        16,
        [VMEM((head, step, 2 * cols), BF16), dma((head,))],
    )(rows, in_hbm(up_weight))
    delta = call(
        functools.partial(delta_kernel, here), shape((batches, OWN_MOST, cols), BF16), "vvvvva"
    )(x, x_other, keep, place, in_vmem(up), acc)
    received = lax.all_to_all(delta, "batch", 0, 0, tiled=True)
    half = shape((requests, cols), F32)
    rest = blocks - head
    mine, send = call(
        functools.partial(base_kernel, step, head, rest),
        [half, half],
        "vvh",
        moves(rest * 4 * step * cols, rest * flops),
        40,
        [
            VMEM((requests, 2 * cols), F32),
            VMEM((12, step, 2 * cols), BF16),
            dma((12,)),
        ],
    )(rows, acc, in_hbm(up_weight))
    return call(final_kernel, shape((requests, cols), BF16), "vvvv")(
        sel, mine, swap(send), received.reshape(batches * OWN_MOST, cols)
    )


def solution(mesh):
    in_specs = (
        P(("group", "batch"), "tensor"),
        P("tensor", "batch"),
        P(("group", "batch"), "tensor", None),
        P(("group", "batch"), "tensor", None),
        P("group"),
        P("group"),
    )
    return jax.shard_map(
        per_device,
        mesh=mesh,
        in_specs=in_specs,
        out_specs=P("group", ("batch", "tensor")),
        check_vma=False,
    )
```

```python
import functools

import jax
import jax.numpy as jnp
from jax import lax
from jax.experimental import pallas as pl
from jax.experimental.pallas import tpu as pltpu
from jax.sharding import PartitionSpec as P

OWN_MOST = 8
LANES = 128
MIB = 1 << 20
F32 = jnp.float32
BF16 = jnp.bfloat16
VMEM = pltpu.VMEM


def whole(n):
    return [pl.BlockSpec(memory_space=VMEM)] * n


def in_vmem(x):
    return pltpu.with_memory_space_constraint(x, VMEM)


def in_hbm(x):
    return pltpu.with_memory_space_constraint(x, pltpu.HBM)


def order_of(batches):
    return sorted(range(batches), key=lambda b: abs(2 * b - batches + 1))


def place_in_order(b, batches):
    return jnp.where(2 * b < batches, batches - 2 - 2 * b, 2 * b - batches + 1)


def exchange(x):
    batches = lax.axis_size("batch")
    return lax.all_to_all(
        x, "batch", 0, 0, tiled=True, axis_index_groups=[order_of(batches)]
    )


def copies_kernel(v_ref, o_ref, sems):
    copies = [
        pltpu.make_async_copy(v_ref, o_ref.at[b], sems.at[b]) for b in range(o_ref.shape[0])
    ]
    for c in copies:
        c.start()
    for c in copies:
        c.wait()


def ready_kernel(
    batches, ra_ref, sr_ref, down_ref, up_ref, upo_ref, keep_ref, place_ref, sel_ref, downv_ref, upv_ref, sems
):
    me = lax.axis_index("batch")
    core = lax.axis_index("tensor")
    rows, hidden = up_ref.shape
    cols = hidden // (2 * batches)
    copies = [pltpu.make_async_copy(down_ref, downv_ref, sems.at[0])]
    for d, b in enumerate(order_of(batches)):
        span = pl.ds(pl.multiple_of((2 * b + core) * cols, LANES), cols)
        for k, ref in enumerate((up_ref, upo_ref)):
            copies.append(
                pltpu.make_async_copy(
                    ref.at[:, span],
                    upv_ref.at[k * rows : (k + 1) * rows, d * cols : (d + 1) * cols],
                    sems.at[1 + 2 * d + k],
                )
            )
    for c in copies:
        c.start()
    requests, adapters = ra_ref.shape[1], sr_ref.shape[1]
    here = adapters // batches

    def iota(shape, dim):
        return lax.broadcasted_iota(jnp.int32, shape, dim)

    square = (requests, requests)
    ra = jnp.sum(jnp.where(iota(square, 0) == iota(square, 1), ra_ref[...], 0), axis=1, keepdims=True)
    slot = jnp.sum(
        jnp.where(iota((requests, adapters), 1) == ra, sr_ref[...], 0), axis=1, keepdims=True
    )
    first = iota((requests, batches), 1) * here
    hit = (slot >= first) & (slot < first + here)
    earlier = jnp.where(iota(square, 1) < iota(square, 0), 1.0, 0.0).astype(BF16)
    marks = jnp.where(hit, 1.0, 0.0)
    counts = jnp.dot(earlier, marks.astype(BF16), preferred_element_type=F32)
    rank = jnp.sum(counts * marks, axis=1, keepdims=True).astype(jnp.int32)
    owner = jnp.sum(jnp.where(hit, iota((requests, batches), 1), 0), axis=1, keepdims=True)
    wide = keep_ref.shape[1]
    width = wide // here
    low = (slot - me * here) * width
    column = iota((requests, wide), 1)
    keep_ref[...] = jnp.where((column >= low) & (column < low + width), 1.0, 0.0)
    mine = (owner == me) & (iota((requests, OWN_MOST), 1) == rank)
    place_ref[...] = jnp.where(mine, 1.0, 0.0).astype(BF16)
    sel_ref[...] = jnp.where(
        iota(sel_ref.shape, 1) == place_in_order(owner, batches) * OWN_MOST + rank, 1.0, 0.0
    ).astype(BF16)
    for c in copies:
        c.wait()


def shrink_kernel(g_ref, down_ref, x_ref, f_ref, rows_ref):
    batches, each, _ = g_ref.shape
    for k, b in enumerate(order_of(batches)):
        rows_ref[b * each : (b + 1) * each] = g_ref[k].astype(F32)
    f_ref[...] = rows_ref[...].astype(BF16)
    x_ref[...] = lax.dot_general(
        f_ref[...], down_ref[...], (((1,), (1,)), ((), ())), preferred_element_type=F32
    )


def delta_kernel(here, x_ref, xo_ref, keep_ref, place_ref, up_ref, acc_ref, d_ref):
    batches, _, cols = d_ref.shape
    core = lax.axis_index("tensor")
    wide = x_ref.shape[1]
    rank = wide // here
    half = rank // 2
    shrunk = (x_ref[...] + xo_ref[...]).astype(BF16)
    kept = (shrunk.astype(F32) * keep_ref[...]).astype(BF16)
    rows = lax.dot_general(
        place_ref[...], kept, (((0,), (0,)), ((), ())), preferred_element_type=F32
    ).astype(BF16)
    i = lax.broadcasted_iota(jnp.int32, (wide, wide), 0)
    j = lax.broadcasted_iota(jnp.int32, (wide, wide), 1)
    side = jnp.where(j < wide // 2, core, 1 - core)
    k = jnp.where(j < wide // 2, j, j - wide // 2)
    source = jnp.zeros_like(k)
    for h in range(here):
        within = (k >= h * half) & (k < (h + 1) * half)
        source = jnp.where(within, h * rank + k - h * half, source)
    pick = jnp.where(i == source + side * half, 1.0, 0.0).astype(BF16)
    rows = jnp.dot(rows, pick, preferred_element_type=F32).astype(BF16)
    for d in range(batches):
        d_ref[d] = jnp.dot(
            rows, up_ref[:, d * cols : (d + 1) * cols], preferred_element_type=F32
        ).astype(BF16)


def stream(step, first, count, f_ref, w_ref, buf, sems, add):
    depth = buf.shape[0]

    def copy(i):
        return pltpu.make_async_copy(
            w_ref.at[pl.ds((first + i) * step, step)], buf.at[i % depth], sems.at[i % depth]
        )

    for i in range(min(depth, count)):
        copy(i).start()
    for i in range(count):
        copy(i).wait()
        k = (first + i) * step
        add(i, jnp.dot(f_ref[:, k : k + step], buf[i % depth], preferred_element_type=F32))
        if i + depth < count:
            copy(i + depth).start()


def head_kernel(step, count, f_ref, w_ref, acc_ref, buf, sems):
    def add(i, part):
        acc_ref[...] = part if i == 0 else acc_ref[...] + part

    stream(step, 0, count, f_ref, w_ref, buf, sems, add)


def base_kernel(own, step, first, count, f_ref, head_ref, w_ref, acc_ref, buf, sems):
    core = lax.axis_index("tensor")
    cols = acc_ref.shape[1]
    side = core if own else 1 - core
    span = pl.ds(pl.multiple_of(side * cols, LANES), cols)

    def add(i, part):
        acc_ref[...] = part + (head_ref[:, span] if i == 0 else acc_ref[...])

    stream(step, first, count, f_ref, w_ref.at[:, span], buf, sems, add)


def final_kernel(sel_ref, keep_ref, got_ref, d_ref, o_ref):
    total = keep_ref[...] + got_ref[...]
    total += jnp.dot(sel_ref[...], d_ref[...], preferred_element_type=F32)
    o_ref[...] = jnp.square(jnp.maximum(total, 0.0)).astype(BF16)


def call(kernel, out, places, cost=None, limit=6, scratch=()):
    spec = {"v": pl.BlockSpec(memory_space=VMEM), "h": pl.BlockSpec(memory_space=pltpu.HBM),
            "a": pl.BlockSpec(memory_space=pl.ANY)}
    many = isinstance(out, (list, tuple))
    return pl.pallas_call(
        kernel,
        out_shape=out,
        in_specs=[spec[p] for p in places],
        out_specs=[spec["v"]] * len(out) if many else spec["v"],
        compiler_params=pltpu.CompilerParams(vmem_limit_bytes=limit * MIB),
        cost_estimate=cost,
        scratch_shapes=scratch,
    )


def moves(size, flops=0):
    return pl.CostEstimate(flops=flops, bytes_accessed=size, transcendentals=0)


def per_device(features, up_weight, down, up, request_adapter, storage_row):
    batches = lax.axis_size("batch")
    here, width, rank = down.shape
    hidden = up.shape[2]
    requests = request_adapter.shape[0]
    cols = up_weight.shape[1] // 2
    wide = here * rank
    shape = jax.ShapeDtypeStruct
    dma = pltpu.SemaphoreType.DMA
    swap = functools.partial(lax.ppermute, axis_name="tensor", perm=[(0, 1), (1, 0)])
    up = up.reshape(-1, hidden)
    up_other = swap(up)
    down = jnp.transpose(down, (0, 2, 1)).reshape(wide, width)
    sent = call(copies_kernel, shape((batches,) + features.shape, BF16), "h", scratch=[dma((batches,))])(in_hbm(features))
    gathered = exchange(sent)
    keep, place, sel, down, up = call(
        functools.partial(ready_kernel, batches),
        [
            shape((requests, wide), F32),
            shape((requests, OWN_MOST), BF16),
            shape((requests, batches * OWN_MOST), BF16),
            VMEM(down.shape, BF16),
            VMEM((wide, hidden // 2), BF16),
        ],
        "vvhha",
        moves(6 * up.size),
        scratch=[dma((1 + 2 * batches,))],
    )(request_adapter.reshape(1, -1), storage_row.reshape(1, -1), in_hbm(down), in_hbm(up), up_other)
    x, rows = call(
        shrink_kernel,
        [shape((requests, wide), F32), shape((requests, width), BF16)],
        "vv",
        scratch=[VMEM((requests, width), F32)],
    )(gathered, in_vmem(down))
    x_other = swap(x)
    step = 256
    head = 1
    blocks = width // step
    flops = 2 * requests * step * 2 * cols
    acc = call(
        functools.partial(head_kernel, step, head),
        shape((requests, 2 * cols), F32),
        "vh",
        moves(head * 4 * step * cols, head * flops),
        16,
        [VMEM((head, step, 2 * cols), BF16), dma((head,))],
    )(rows, in_hbm(up_weight))
    delta = call(
        functools.partial(delta_kernel, here), shape((batches, OWN_MOST, cols), BF16), "vvvvva"
    )(x, x_other, keep, place, in_vmem(up), acc)
    received = exchange(delta)
    rest = blocks - head

    def base(own):
        return call(
            functools.partial(base_kernel, own, step, head, rest),
            shape((requests, cols), F32),
            "vvh",
            moves(rest * 2 * step * cols, rest * flops // 2),
            40,
            [VMEM((min(15, rest), step, cols), BF16), dma((min(15, rest),))],
        )(rows, acc, in_hbm(up_weight))

    other = swap(base(False))
    mine = base(True)
    return call(final_kernel, shape((requests, cols), BF16), "vvvv")(
        sel, mine, other, received.reshape(batches * OWN_MOST, cols)
    )


def solution(mesh):
    in_specs = (
        P(("group", "batch"), "tensor"),
        P("tensor", "batch"),
        P(("group", "batch"), "tensor", None),
        P(("group", "batch"), "tensor", None),
        P("group"),
        P("group"),
    )
    return jax.shard_map(
        per_device,
        mesh=mesh,
        in_specs=in_specs,
        out_specs=P("group", ("batch", "tensor")),
        check_vma=False,
    )
```

```python
import functools

import jax
import jax.numpy as jnp
from jax import lax
from jax.experimental import pallas as pl
from jax.experimental.pallas import tpu as pltpu
from jax.sharding import PartitionSpec as P

OWN_MOST = 8
LANES = 128
MIB = 1 << 20
F32 = jnp.float32
BF16 = jnp.bfloat16
VMEM = pltpu.VMEM


def whole(n):
    return [pl.BlockSpec(memory_space=VMEM)] * n


def in_vmem(x):
    return pltpu.with_memory_space_constraint(x, VMEM)


def in_hbm(x):
    return pltpu.with_memory_space_constraint(x, pltpu.HBM)


def order_of(batches):
    return sorted(range(batches), key=lambda b: abs(2 * b - batches + 1))


def place_in_order(b, batches):
    return jnp.where(2 * b < batches, batches - 2 - 2 * b, 2 * b - batches + 1)


def exchange(x):
    batches = lax.axis_size("batch")
    return lax.all_to_all(
        x, "batch", 0, 0, tiled=True, axis_index_groups=[order_of(batches)]
    )


def columns(batches, ref, out, sems):
    core = lax.axis_index("tensor")
    cols = out.shape[1] // batches
    return [
        pltpu.make_async_copy(
            ref.at[:, pl.ds(pl.multiple_of((2 * b + core) * cols, LANES), cols)],
            out.at[:, d * cols : (d + 1) * cols],
            sems.at[d],
        )
        for d, b in enumerate(order_of(batches))
    ]


def ready_kernel(
    batches, ra_ref, sr_ref, down_ref, up_ref, keep_ref, place_ref, sel_ref, downv_ref, upv_ref, sems
):
    me = lax.axis_index("batch")
    copies = [pltpu.make_async_copy(down_ref, downv_ref, sems.at[batches])]
    copies += columns(batches, up_ref, upv_ref, sems)
    for c in copies:
        c.start()
    requests, adapters = ra_ref.shape[1], sr_ref.shape[1]
    here = adapters // batches

    def iota(shape, dim):
        return lax.broadcasted_iota(jnp.int32, shape, dim)

    square = (requests, requests)
    ra = jnp.sum(jnp.where(iota(square, 0) == iota(square, 1), ra_ref[...], 0), axis=1, keepdims=True)
    slot = jnp.sum(
        jnp.where(iota((requests, adapters), 1) == ra, sr_ref[...], 0), axis=1, keepdims=True
    )
    first = iota((requests, batches), 1) * here
    hit = (slot >= first) & (slot < first + here)
    earlier = jnp.where(iota(square, 1) < iota(square, 0), 1.0, 0.0).astype(BF16)
    marks = jnp.where(hit, 1.0, 0.0)
    counts = jnp.dot(earlier, marks.astype(BF16), preferred_element_type=F32)
    rank = jnp.sum(counts * marks, axis=1, keepdims=True).astype(jnp.int32)
    owner = jnp.sum(jnp.where(hit, iota((requests, batches), 1), 0), axis=1, keepdims=True)
    wide = keep_ref.shape[1]
    width = wide // here
    low = (slot - me * here) * width
    column = iota((requests, wide), 1)
    keep_ref[...] = jnp.where((column >= low) & (column < low + width), 1.0, 0.0)
    mine = (owner == me) & (iota((requests, OWN_MOST), 1) == rank)
    place_ref[...] = jnp.where(mine, 1.0, 0.0).astype(BF16)
    sel_ref[...] = jnp.where(
        iota(sel_ref.shape, 1) == place_in_order(owner, batches) * OWN_MOST + rank, 1.0, 0.0
    ).astype(BF16)
    for c in copies:
        c.wait()


def shrink_kernel(g_ref, down_ref, x_ref, f_ref, rows_ref):
    batches, each, _ = g_ref.shape
    for k, b in enumerate(order_of(batches)):
        rows_ref[b * each : (b + 1) * each] = g_ref[k].astype(F32)
    f_ref[...] = rows_ref[...].astype(BF16)
    x_ref[...] = lax.dot_general(
        f_ref[...], down_ref[...], (((1,), (1,)), ((), ())), preferred_element_type=F32
    )


def delta_kernel(
    here, step, first, x_ref, xo_ref, keep_ref, place_ref, upa_ref, upb_ref, f_ref, head_ref, w_ref,
    out_ref, acc_ref, next_ref, d_ref, buf, sems, out_sems
):
    taken = pltpu.make_async_copy(w_ref.at[pl.ds(first * step, step)], buf, sems.at[0])
    coming = pltpu.make_async_copy(w_ref.at[pl.ds((first + 1) * step, step)], next_ref, sems.at[1])
    taken.start()
    coming.start()
    batches, _, cols = d_ref.shape
    core = lax.axis_index("tensor")
    wide = x_ref.shape[1]
    rank = wide // here
    half = rank // 2
    shrunk = (x_ref[...] + xo_ref[...]).astype(BF16)
    kept = (shrunk.astype(F32) * keep_ref[...]).astype(BF16)
    rows = lax.dot_general(
        place_ref[...], kept, (((0,), (0,)), ((), ())), preferred_element_type=F32
    ).astype(BF16)
    i = lax.broadcasted_iota(jnp.int32, (wide, wide // 2), 0)
    k = lax.broadcasted_iota(jnp.int32, (wide, wide // 2), 1)
    source = jnp.zeros_like(k)
    for h in range(here):
        within = (k >= h * half) & (k < (h + 1) * half)
        source = jnp.where(within, h * rank + k - h * half, source)

    def part(side):
        pick = jnp.where(i == source + side * half, 1.0, 0.0).astype(BF16)
        return jnp.dot(rows, pick, preferred_element_type=F32).astype(BF16)

    def out(d):
        return pltpu.make_async_copy(d_ref.at[d], out_ref.at[d], out_sems.at[d])

    own, other = part(core), part(1 - core)
    for d in range(batches):
        span = slice(d * cols, (d + 1) * cols)
        total = jnp.dot(own, upa_ref[:, span], preferred_element_type=F32)
        total += jnp.dot(other, upb_ref[:, span], preferred_element_type=F32)
        d_ref[d] = total.astype(BF16)
        out(d).start()
    taken.wait()
    k = first * step
    acc_ref[...] = head_ref[...] + jnp.dot(
        f_ref[:, k : k + step], buf[...], preferred_element_type=F32
    )
    coming.wait()
    for d in range(batches):
        out(d).wait()


def stream(step, first, count, f_ref, w_ref, buf, sems, add):
    depth = buf.shape[0]

    def copy(i):
        return pltpu.make_async_copy(
            w_ref.at[pl.ds((first + i) * step, step)], buf.at[i % depth], sems.at[i % depth]
        )

    for i in range(min(depth, count)):
        copy(i).start()
    for i in range(count):
        copy(i).wait()
        k = (first + i) * step
        add(i, jnp.dot(f_ref[:, k : k + step], buf[i % depth], preferred_element_type=F32))
        if i + depth < count:
            copy(i + depth).start()


def head_kernel(batches, step, count, f_ref, w_ref, up_ref, acc_ref, upv_ref, buf, sems, upsems):
    copies = columns(batches, up_ref, upv_ref, upsems)
    for c in copies:
        c.start()

    def add(i, part):
        acc_ref[...] = part if i == 0 else acc_ref[...] + part

    stream(step, 0, count, f_ref, w_ref, buf, sems, add)
    for c in copies:
        c.wait()


def base_kernel(own, step, first, count, f_ref, head_ref, here_ref, w_ref, acc_ref, buf, sems):
    core = lax.axis_index("tensor")
    cols = acc_ref.shape[1]
    side = core if own else 1 - core
    span = pl.ds(pl.multiple_of(side * cols, LANES), cols)

    def copy(i):
        k = (first + 1 + i) * step
        return pltpu.make_async_copy(w_ref.at[k : k + step, span], buf.at[i], sems.at[i])

    for i in range(count):
        copy(i).start()
    k = first * step
    acc_ref[...] = head_ref[:, span] + jnp.dot(
        f_ref[:, k : k + step], here_ref[:, span], preferred_element_type=F32
    )
    for i in range(count):
        copy(i).wait()
        k = (first + 1 + i) * step
        acc_ref[...] += jnp.dot(f_ref[:, k : k + step], buf[i], preferred_element_type=F32)


def final_kernel(sel_ref, keep_ref, got_ref, d_ref, o_ref):
    total = keep_ref[...] + got_ref[...]
    total += jnp.dot(sel_ref[...], d_ref[...], preferred_element_type=F32)
    o_ref[...] = jnp.square(jnp.maximum(total, 0.0)).astype(BF16)


def call(kernel, out, places, cost=None, limit=6, scratch=(), outs=None):
    spec = {"v": pl.BlockSpec(memory_space=VMEM), "h": pl.BlockSpec(memory_space=pltpu.HBM),
            "a": pl.BlockSpec(memory_space=pl.ANY)}
    many = isinstance(out, (list, tuple))
    return pl.pallas_call(
        kernel,
        out_shape=out,
        in_specs=[spec[p] for p in places],
        out_specs=[spec[p] for p in outs or "v" * len(out)] if many else spec["v"],
        compiler_params=pltpu.CompilerParams(vmem_limit_bytes=limit * MIB),
        cost_estimate=cost,
        scratch_shapes=scratch,
    )


def moves(size, flops=0):
    return pl.CostEstimate(flops=flops, bytes_accessed=size, transcendentals=0)


def per_device(features, up_weight, down, up, request_adapter, storage_row):
    batches = lax.axis_size("batch")
    here, width, rank = down.shape
    hidden = up.shape[2]
    requests = request_adapter.shape[0]
    cols = up_weight.shape[1] // 2
    wide = here * rank
    shape = jax.ShapeDtypeStruct
    dma = pltpu.SemaphoreType.DMA
    swap = functools.partial(lax.ppermute, axis_name="tensor", perm=[(0, 1), (1, 0)])
    down = jnp.transpose(down, (0, 2, 1)).reshape(wide, width)
    sent = jnp.broadcast_to(features[None], (batches,) + features.shape)
    sent, up = lax.optimization_barrier((sent, up.reshape(-1, hidden)))
    up_other = swap(up)
    gathered = exchange(sent)
    keep, place, sel, down, up_b = call(
        functools.partial(ready_kernel, batches),
        [
            shape((requests, wide), F32),
            shape((requests, OWN_MOST), BF16),
            shape((requests, batches * OWN_MOST), BF16),
            VMEM(down.shape, BF16),
            VMEM((wide // 2, hidden // 2), BF16),
        ],
        "vvhh",
        moves(6 * up.size),
        scratch=[dma((1 + batches,))],
    )(request_adapter.reshape(1, -1), storage_row.reshape(1, -1), in_hbm(down), in_hbm(up_other))
    x, rows = call(
        shrink_kernel,
        [shape((requests, wide), F32), shape((requests, width), BF16)],
        "vv",
        scratch=[VMEM((requests, width), F32)],
    )(gathered, in_vmem(down))
    x_other = swap(x)
    step = 256
    head = 1
    blocks = width // step
    flops = 2 * requests * step * 2 * cols
    total = shape((requests, 2 * cols), F32)
    acc, up_a = call(
        functools.partial(head_kernel, batches, step, head),
        [total, VMEM((wide // 2, hidden // 2), BF16)],
        "vhh",
        moves(head * 4 * step * cols, head * flops),
        16,
        [VMEM((head, step, 2 * cols), BF16), dma((head,)), dma((batches,))],
    )(rows, in_hbm(up_weight), in_hbm(up))
    delta, acc, ahead = call(
        functools.partial(delta_kernel, here, step, head),
        [pltpu.HBM((batches, OWN_MOST, cols), BF16), total, VMEM((step, 2 * cols), BF16)],
        "vvvvvvvvh",
        scratch=[
            VMEM((batches, OWN_MOST, cols), BF16),
            VMEM((step, 2 * cols), BF16),
            dma((2,)),
            dma((batches,)),
        ],
        outs="hvv",
    )(x, x_other, keep, place, in_vmem(up_a), in_vmem(up_b), rows, acc, in_hbm(up_weight))
    received = exchange(delta)
    rest = blocks - head - 2

    def base(own):
        return call(
            functools.partial(base_kernel, own, step, head + 1, rest),
            shape((requests, cols), F32),
            "vvvh",
            moves(rest * 2 * step * cols, rest * flops // 2),
            24,
            [VMEM((rest, step, cols), BF16), dma((rest,))],
        )(rows, acc, in_vmem(ahead), in_hbm(up_weight))

    other = swap(base(False))
    mine = base(True)
    return call(final_kernel, shape((requests, cols), BF16), "vvvv")(
        sel, mine, other, received.reshape(batches * OWN_MOST, cols)
    )


def solution(mesh):
    in_specs = (
        P(("group", "batch"), "tensor"),
        P("tensor", "batch"),
        P(("group", "batch"), "tensor", None),
        P(("group", "batch"), "tensor", None),
        P("group"),
        P("group"),
    )
    return jax.shard_map(
        per_device,
        mesh=mesh,
        in_specs=in_specs,
        out_specs=P("group", ("batch", "tensor")),
        check_vma=False,
    )
```

```python
import functools

import jax
import jax.numpy as jnp
from jax import lax
from jax.experimental import pallas as pl
from jax.experimental.pallas import tpu as pltpu
from jax.sharding import PartitionSpec as P

OWN_MOST = 8
LANES = 128
MIB = 1 << 20
F32 = jnp.float32
BF16 = jnp.bfloat16
VMEM = pltpu.VMEM


def whole(n):
    return [pl.BlockSpec(memory_space=VMEM)] * n


def in_vmem(x):
    return pltpu.with_memory_space_constraint(x, VMEM)


def in_hbm(x):
    return pltpu.with_memory_space_constraint(x, pltpu.HBM)


def order_of(batches):
    return sorted(range(batches), key=lambda b: abs(2 * b - batches + 1))


def place_in_order(b, batches):
    return jnp.where(2 * b < batches, batches - 2 - 2 * b, 2 * b - batches + 1)


def exchange(x):
    batches = lax.axis_size("batch")
    return lax.all_to_all(
        x, "batch", 0, 0, tiled=True, axis_index_groups=[order_of(batches)]
    )


def ready_kernel(
    batches, ra_in, sr_in, down_ref, up_ref, upo_ref, w_ref,
    keep_ref, place_ref, sel_ref, downv_ref, upv_ref, wv_ref, ra_ref, sr_ref, sems, index_sems
):
    me = lax.axis_index("batch")
    core = lax.axis_index("tensor")
    rows, hidden = up_ref.shape
    cols = hidden // (2 * batches)
    copies = [
        pltpu.make_async_copy(down_ref, downv_ref, sems.at[0]),
        pltpu.make_async_copy(w_ref.at[: wv_ref.shape[0]], wv_ref, sems.at[2 * batches + 1]),
    ]
    for d, b in enumerate(order_of(batches)):
        span = pl.ds(pl.multiple_of((2 * b + core) * cols, LANES), cols)
        for k, ref in enumerate((up_ref, upo_ref)):
            copies.append(
                pltpu.make_async_copy(
                    ref.at[:, span],
                    upv_ref.at[k * rows : (k + 1) * rows, d * cols : (d + 1) * cols],
                    sems.at[1 + 2 * d + k],
                )
            )
    indices = [
        pltpu.make_async_copy(ra_in, ra_ref, index_sems.at[0]),
        pltpu.make_async_copy(sr_in, sr_ref, index_sems.at[1]),
    ]
    for c in indices + copies:
        c.start()
    for c in indices:
        c.wait()
    requests, adapters = ra_ref.shape[1], sr_ref.shape[1]
    here = adapters // batches

    def iota(shape, dim):
        return lax.broadcasted_iota(jnp.int32, shape, dim)

    square = (requests, requests)
    ra = jnp.sum(jnp.where(iota(square, 0) == iota(square, 1), ra_ref[...], 0), axis=1, keepdims=True)
    slot = jnp.sum(
        jnp.where(iota((requests, adapters), 1) == ra, sr_ref[...], 0), axis=1, keepdims=True
    )
    first = iota((requests, batches), 1) * here
    hit = (slot >= first) & (slot < first + here)
    earlier = jnp.where(iota(square, 1) < iota(square, 0), 1.0, 0.0).astype(BF16)
    marks = jnp.where(hit, 1.0, 0.0)
    counts = jnp.dot(earlier, marks.astype(BF16), preferred_element_type=F32)
    rank = jnp.sum(counts * marks, axis=1, keepdims=True).astype(jnp.int32)
    owner = jnp.sum(jnp.where(hit, iota((requests, batches), 1), 0), axis=1, keepdims=True)
    wide = keep_ref.shape[1]
    width = wide // here
    low = (slot - me * here) * width
    column = iota((requests, wide), 1)
    keep_ref[...] = jnp.where((column >= low) & (column < low + width), 1.0, 0.0)
    mine = (owner == me) & (iota((requests, OWN_MOST), 1) == rank)
    place_ref[...] = jnp.where(mine, 1.0, 0.0).astype(BF16)
    sel_ref[...] = jnp.where(
        iota(sel_ref.shape, 1) == place_in_order(owner, batches) * OWN_MOST + rank, 1.0, 0.0
    ).astype(BF16)
    for c in copies:
        c.wait()


def shrink_kernel(g_ref, down_ref, x_ref, f_ref, rows_ref):
    batches, each, _ = g_ref.shape
    for k, b in enumerate(order_of(batches)):
        rows_ref[b * each : (b + 1) * each] = g_ref[k].astype(F32)
    f_ref[...] = rows_ref[...].astype(BF16)
    x_ref[...] = lax.dot_general(
        f_ref[...], down_ref[...], (((1,), (1,)), ((), ())), preferred_element_type=F32
    )


def delta_kernel(here, x_ref, xo_ref, keep_ref, place_ref, up_ref, acc_ref, out_ref, d_ref, sems):
    batches, _, cols = d_ref.shape
    core = lax.axis_index("tensor")
    wide = x_ref.shape[1]
    rank = wide // here
    half = rank // 2
    shrunk = (x_ref[...] + xo_ref[...]).astype(BF16)
    kept = (shrunk.astype(F32) * keep_ref[...]).astype(BF16)
    rows = lax.dot_general(
        place_ref[...], kept, (((0,), (0,)), ((), ())), preferred_element_type=F32
    ).astype(BF16)
    i = lax.broadcasted_iota(jnp.int32, (wide, wide), 0)
    j = lax.broadcasted_iota(jnp.int32, (wide, wide), 1)
    side = jnp.where(j < wide // 2, core, 1 - core)
    k = jnp.where(j < wide // 2, j, j - wide // 2)
    source = jnp.zeros_like(k)
    for h in range(here):
        within = (k >= h * half) & (k < (h + 1) * half)
        source = jnp.where(within, h * rank + k - h * half, source)
    pick = jnp.where(i == source + side * half, 1.0, 0.0).astype(BF16)
    rows = jnp.dot(rows, pick, preferred_element_type=F32).astype(BF16)
    copies = []
    for d in range(batches):
        d_ref[d] = jnp.dot(
            rows, up_ref[:, d * cols : (d + 1) * cols], preferred_element_type=F32
        ).astype(BF16)
        copies.append(pltpu.make_async_copy(d_ref.at[d], out_ref.at[d], sems.at[d]))
        copies[d].start()
    for c in copies:
        c.wait()


def stream(step, first, count, f_ref, w_ref, buf, sems, add):
    depth = buf.shape[0]

    def copy(i):
        return pltpu.make_async_copy(
            w_ref.at[pl.ds((first + i) * step, step)], buf.at[i % depth], sems.at[i % depth]
        )

    for i in range(min(depth, count)):
        copy(i).start()
    for i in range(count):
        copy(i).wait()
        k = (first + i) * step
        add(i, jnp.dot(f_ref[:, k : k + step], buf[i % depth], preferred_element_type=F32))
        if i + depth < count:
            copy(i + depth).start()


def head_kernel(f_ref, w_ref, acc_ref):
    acc_ref[...] = jnp.dot(
        f_ref[:, : w_ref.shape[0]], w_ref[...], preferred_element_type=F32
    )


def base_kernel(own, step, first, count, f_ref, head_ref, w_ref, acc_ref, buf, sems):
    core = lax.axis_index("tensor")
    cols = acc_ref.shape[1]
    side = core if own else 1 - core
    span = pl.ds(pl.multiple_of(side * cols, LANES), cols)

    def add(i, part):
        acc_ref[...] = part + (head_ref[:, span] if i == 0 else acc_ref[...])

    stream(step, first, count, f_ref, w_ref.at[:, span], buf, sems, add)


def final_kernel(sel_ref, keep_ref, got_ref, d_ref, o_ref):
    total = keep_ref[...] + got_ref[...]
    total += jnp.dot(sel_ref[...], d_ref[...], preferred_element_type=F32)
    o_ref[...] = jnp.square(jnp.maximum(total, 0.0)).astype(BF16)


def call(kernel, out, places, cost=None, limit=6, scratch=(), outs=None):
    spec = {"v": pl.BlockSpec(memory_space=VMEM), "h": pl.BlockSpec(memory_space=pltpu.HBM),
            "a": pl.BlockSpec(memory_space=pl.ANY)}
    many = isinstance(out, (list, tuple))
    return pl.pallas_call(
        kernel,
        out_shape=out,
        in_specs=[spec[p] for p in places],
        out_specs=[spec[p] for p in outs or "v" * len(out)] if many else spec["v"],
        compiler_params=pltpu.CompilerParams(vmem_limit_bytes=limit * MIB),
        cost_estimate=cost,
        scratch_shapes=scratch,
    )


def moves(size, flops=0):
    return pl.CostEstimate(flops=flops, bytes_accessed=size, transcendentals=0)


def per_device(features, up_weight, down, up, request_adapter, storage_row):
    batches = lax.axis_size("batch")
    here, width, rank = down.shape
    hidden = up.shape[2]
    requests = request_adapter.shape[0]
    cols = up_weight.shape[1] // 2
    wide = here * rank
    shape = jax.ShapeDtypeStruct
    dma = pltpu.SemaphoreType.DMA
    swap = functools.partial(lax.ppermute, axis_name="tensor", perm=[(0, 1), (1, 0)])
    up = up.reshape(-1, hidden)
    up_other = swap(up)
    down = jnp.transpose(down, (0, 2, 1)).reshape(wide, width)
    sent = jnp.broadcast_to(features[None], (batches,) + features.shape)
    gathered = exchange(sent)
    step = 256
    head = 1
    keep, place, sel, down, up, first = call(
        functools.partial(ready_kernel, batches),
        [
            shape((requests, wide), F32),
            shape((requests, OWN_MOST), BF16),
            shape((requests, batches * OWN_MOST), BF16),
            VMEM(down.shape, BF16),
            VMEM((wide, hidden // 2), BF16),
            VMEM((head * step, 2 * cols), BF16),
        ],
        "hhhhhh",
        moves(6 * up.size),
        scratch=[
            VMEM((1, requests), jnp.int32),
            VMEM((1, storage_row.shape[0]), jnp.int32),
            dma((2 + 2 * batches,)),
            dma((2,)),
        ],
    )(
        in_hbm(request_adapter.reshape(1, -1)),
        in_hbm(storage_row.reshape(1, -1)),
        in_hbm(down),
        in_hbm(up),
        in_hbm(up_other),
        in_hbm(up_weight),
    )
    x, rows = call(
        shrink_kernel,
        [shape((requests, wide), F32), shape((requests, width), BF16)],
        "vv",
        scratch=[VMEM((requests, width), F32)],
    )(gathered, in_vmem(down))
    x_other = swap(x)
    blocks = width // step
    flops = 2 * requests * step * 2 * cols
    acc = call(
        head_kernel,
        shape((requests, 2 * cols), F32),
        "vv",
        moves(head * 4 * step * cols, head * flops),
    )(rows, in_vmem(first))
    (delta,) = call(
        functools.partial(delta_kernel, here),
        [pltpu.HBM((batches, OWN_MOST, cols), BF16)],
        "vvvvva",
        scratch=[VMEM((batches, OWN_MOST, cols), BF16), dma((batches,))],
        outs="h",
    )(x, x_other, keep, place, in_vmem(up), acc)
    received = exchange(delta)
    rest = blocks - head

    def base(own):
        return call(
            functools.partial(base_kernel, own, step, head, rest),
            shape((requests, cols), F32),
            "vvh",
            moves(rest * 2 * step * cols, rest * flops // 2),
            40,
            [VMEM((min(15, rest), step, cols), BF16), dma((min(15, rest),))],
        )(rows, acc, in_hbm(up_weight))

    other = swap(base(False))
    mine = base(True)
    return call(final_kernel, shape((requests, cols), BF16), "vvvv")(
        sel, mine, other, received.reshape(batches * OWN_MOST, cols)
    )


def solution(mesh):
    in_specs = (
        P(("group", "batch"), "tensor"),
        P("tensor", "batch"),
        P(("group", "batch"), "tensor", None),
        P(("group", "batch"), "tensor", None),
        P("group"),
        P("group"),
    )
    return jax.shard_map(
        per_device,
        mesh=mesh,
        in_specs=in_specs,
        out_specs=P("group", ("batch", "tensor")),
        check_vma=False,
    )
```

```python
import functools

import jax
import jax.numpy as jnp
from jax import lax
from jax.experimental import pallas as pl
from jax.experimental.pallas import tpu as pltpu
from jax.sharding import PartitionSpec as P

OWN_MOST = 8
LANES = 128
MIB = 1 << 20
F32 = jnp.float32
BF16 = jnp.bfloat16
VMEM = pltpu.VMEM


def whole(n):
    return [pl.BlockSpec(memory_space=VMEM)] * n


def in_vmem(x):
    return pltpu.with_memory_space_constraint(x, VMEM)


def in_hbm(x):
    return pltpu.with_memory_space_constraint(x, pltpu.HBM)


def order_of(batches):
    return sorted(range(batches), key=lambda b: abs(2 * b - batches + 1))


def place_in_order(b, batches):
    return jnp.where(2 * b < batches, batches - 2 - 2 * b, 2 * b - batches + 1)


def exchange(x):
    batches = lax.axis_size("batch")
    return lax.all_to_all(
        x, "batch", 0, 0, tiled=True, axis_index_groups=[order_of(batches)]
    )


def ready_kernel(
    batches, ra_in, sr_in, down_ref, up_ref, upo_ref, w_ref,
    keep_ref, place_ref, sel_ref, downv_ref, upv_ref, wv_ref, ra_ref, sr_ref, stage, sems, index_sems
):
    me = lax.axis_index("batch")
    core = lax.axis_index("tensor")
    rows, hidden = up_ref.shape
    cols = hidden // (2 * batches)
    last = [
        pltpu.make_async_copy(down_ref, downv_ref, sems.at[0]),
        pltpu.make_async_copy(w_ref.at[: wv_ref.shape[0]], wv_ref, sems.at[2 * batches + 1]),
    ]
    copies = []
    for d, b in enumerate(order_of(batches)):
        span = pl.ds(pl.multiple_of((2 * b + core) * cols, LANES), cols)
        for k, ref in enumerate((up_ref, upo_ref)):
            copies.append(
                pltpu.make_async_copy(
                    ref.at[:, span],
                    stage.at[k * rows : (k + 1) * rows, d * cols : (d + 1) * cols],
                    sems.at[1 + 2 * d + k],
                )
            )
    indices = [
        pltpu.make_async_copy(ra_in, ra_ref, index_sems.at[0]),
        pltpu.make_async_copy(sr_in, sr_ref, index_sems.at[1]),
    ]
    for c in indices + copies + last:
        c.start()
    for c in indices:
        c.wait()
    requests, adapters = ra_ref.shape[1], sr_ref.shape[1]
    here = adapters // batches

    def iota(shape, dim):
        return lax.broadcasted_iota(jnp.int32, shape, dim)

    square = (requests, requests)
    ra = jnp.sum(jnp.where(iota(square, 0) == iota(square, 1), ra_ref[...], 0), axis=1, keepdims=True)
    slot = jnp.sum(
        jnp.where(iota((requests, adapters), 1) == ra, sr_ref[...], 0), axis=1, keepdims=True
    )
    first = iota((requests, batches), 1) * here
    hit = (slot >= first) & (slot < first + here)
    earlier = jnp.where(iota(square, 1) < iota(square, 0), 1.0, 0.0).astype(BF16)
    marks = jnp.where(hit, 1.0, 0.0)
    counts = jnp.dot(earlier, marks.astype(BF16), preferred_element_type=F32)
    rank = jnp.sum(counts * marks, axis=1, keepdims=True).astype(jnp.int32)
    owner = jnp.sum(jnp.where(hit, iota((requests, batches), 1), 0), axis=1, keepdims=True)
    wide = keep_ref.shape[1]
    width = wide // here
    low = (slot - me * here) * width
    column = iota((requests, wide), 1)
    keep_ref[...] = jnp.where((column >= low) & (column < low + width), 1.0, 0.0)
    mine = (owner == me) & (iota((requests, OWN_MOST), 1) == rank)
    place_ref[...] = jnp.where(mine, 1.0, 0.0).astype(BF16)
    sel_ref[...] = jnp.where(
        iota(sel_ref.shape, 1) == place_in_order(owner, batches) * OWN_MOST + rank, 1.0, 0.0
    ).astype(BF16)
    for c in copies:
        c.wait()
    back = pltpu.make_async_copy(stage, upv_ref, sems.at[2 * batches + 2])
    back.start()
    for c in last + [back]:
        c.wait()


def shrink_kernel(g_ref, down_ref, x_ref, f_ref, rows_ref):
    batches, each, _ = g_ref.shape
    for k, b in enumerate(order_of(batches)):
        rows_ref[b * each : (b + 1) * each] = g_ref[k].astype(F32)
    f_ref[...] = rows_ref[...].astype(BF16)
    x_ref[...] = lax.dot_general(
        f_ref[...], down_ref[...], (((1,), (1,)), ((), ())), preferred_element_type=F32
    )


def delta_kernel(here, x_ref, xo_ref, keep_ref, place_ref, up_ref, acc_ref, out_ref, d_ref, sems):
    batches, _, cols = d_ref.shape
    core = lax.axis_index("tensor")
    wide = x_ref.shape[1]
    rank = wide // here
    half = rank // 2
    shrunk = (x_ref[...] + xo_ref[...]).astype(BF16)
    kept = (shrunk.astype(F32) * keep_ref[...]).astype(BF16)
    rows = lax.dot_general(
        place_ref[...], kept, (((0,), (0,)), ((), ())), preferred_element_type=F32
    ).astype(BF16)
    i = lax.broadcasted_iota(jnp.int32, (wide, wide), 0)
    j = lax.broadcasted_iota(jnp.int32, (wide, wide), 1)
    side = jnp.where(j < wide // 2, core, 1 - core)
    k = jnp.where(j < wide // 2, j, j - wide // 2)
    source = jnp.zeros_like(k)
    for h in range(here):
        within = (k >= h * half) & (k < (h + 1) * half)
        source = jnp.where(within, h * rank + k - h * half, source)
    pick = jnp.where(i == source + side * half, 1.0, 0.0).astype(BF16)
    rows = jnp.dot(rows, pick, preferred_element_type=F32).astype(BF16)
    copies = []
    for d in range(batches):
        d_ref[d] = jnp.dot(
            rows, up_ref[:, d * cols : (d + 1) * cols], preferred_element_type=F32
        ).astype(BF16)
        copies.append(pltpu.make_async_copy(d_ref.at[d], out_ref.at[d], sems.at[d]))
        copies[d].start()
    for c in copies:
        c.wait()


def stream(step, first, count, f_ref, w_ref, buf, sems, add):
    depth = buf.shape[0]

    def copy(i):
        return pltpu.make_async_copy(
            w_ref.at[pl.ds((first + i) * step, step)], buf.at[i % depth], sems.at[i % depth]
        )

    for i in range(min(depth, count)):
        copy(i).start()
    for i in range(count):
        copy(i).wait()
        k = (first + i) * step
        add(i, jnp.dot(f_ref[:, k : k + step], buf[i % depth], preferred_element_type=F32))
        if i + depth < count:
            copy(i + depth).start()


def head_kernel(f_ref, w_ref, acc_ref):
    acc_ref[...] = jnp.dot(
        f_ref[:, : w_ref.shape[0]], w_ref[...], preferred_element_type=F32
    )


def base_kernel(own, step, first, count, f_ref, head_ref, w_ref, acc_ref, buf, sems):
    core = lax.axis_index("tensor")
    cols = acc_ref.shape[1]
    side = core if own else 1 - core
    span = pl.ds(pl.multiple_of(side * cols, LANES), cols)

    def add(i, part):
        acc_ref[...] = part + (head_ref[:, span] if i == 0 else acc_ref[...])

    stream(step, first, count, f_ref, w_ref.at[:, span], buf, sems, add)


def final_kernel(sel_ref, keep_ref, got_ref, d_ref, o_ref):
    total = keep_ref[...] + got_ref[...]
    total += jnp.dot(sel_ref[...], d_ref[...], preferred_element_type=F32)
    o_ref[...] = jnp.square(jnp.maximum(total, 0.0)).astype(BF16)


def call(kernel, out, places, cost=None, limit=6, scratch=(), outs=None):
    spec = {"v": pl.BlockSpec(memory_space=VMEM), "h": pl.BlockSpec(memory_space=pltpu.HBM),
            "a": pl.BlockSpec(memory_space=pl.ANY)}
    many = isinstance(out, (list, tuple))
    return pl.pallas_call(
        kernel,
        out_shape=out,
        in_specs=[spec[p] for p in places],
        out_specs=[spec[p] for p in outs or "v" * len(out)] if many else spec["v"],
        compiler_params=pltpu.CompilerParams(vmem_limit_bytes=limit * MIB),
        cost_estimate=cost,
        scratch_shapes=scratch,
    )


def moves(size, flops=0):
    return pl.CostEstimate(flops=flops, bytes_accessed=size, transcendentals=0)


def per_device(features, up_weight, down, up, request_adapter, storage_row):
    batches = lax.axis_size("batch")
    here, width, rank = down.shape
    hidden = up.shape[2]
    requests = request_adapter.shape[0]
    cols = up_weight.shape[1] // 2
    wide = here * rank
    shape = jax.ShapeDtypeStruct
    dma = pltpu.SemaphoreType.DMA
    swap = functools.partial(lax.ppermute, axis_name="tensor", perm=[(0, 1), (1, 0)])
    up = up.reshape(-1, hidden)
    up_other = swap(up)
    down = jnp.transpose(down, (0, 2, 1)).reshape(wide, width)
    sent = jnp.broadcast_to(features[None], (batches,) + features.shape)
    gathered = exchange(sent)
    step = 256
    head = 1
    keep, place, sel, down, up, first = call(
        functools.partial(ready_kernel, batches),
        [
            shape((requests, wide), F32),
            shape((requests, OWN_MOST), BF16),
            shape((requests, batches * OWN_MOST), BF16),
            VMEM(down.shape, BF16),
            pltpu.HBM((wide, hidden // 2), BF16),
            VMEM((head * step, 2 * cols), BF16),
        ],
        "hhhhhh",
        moves(6 * up.size),
        scratch=[
            VMEM((1, requests), jnp.int32),
            VMEM((1, storage_row.shape[0]), jnp.int32),
            VMEM((wide, hidden // 2), BF16),
            dma((3 + 2 * batches,)),
            dma((2,)),
        ],
        outs="vvvvhv",
    )(
        in_hbm(request_adapter.reshape(1, -1)),
        in_hbm(storage_row.reshape(1, -1)),
        in_hbm(down),
        in_hbm(up),
        in_hbm(up_other),
        in_hbm(up_weight),
    )
    x, rows = call(
        shrink_kernel,
        [shape((requests, wide), F32), shape((requests, width), BF16)],
        "vv",
        scratch=[VMEM((requests, width), F32)],
    )(gathered, in_vmem(down))
    x_other = swap(x)
    blocks = width // step
    flops = 2 * requests * step * 2 * cols
    acc = call(
        head_kernel,
        shape((requests, 2 * cols), F32),
        "vv",
        moves(head * 4 * step * cols, head * flops),
    )(rows, in_vmem(first))
    (delta,) = call(
        functools.partial(delta_kernel, here),
        [pltpu.HBM((batches, OWN_MOST, cols), BF16)],
        "vvvvva",
        scratch=[VMEM((batches, OWN_MOST, cols), BF16), dma((batches,))],
        outs="h",
    )(x, x_other, keep, place, up, acc)
    received = exchange(delta)
    rest = blocks - head

    def base(own):
        return call(
            functools.partial(base_kernel, own, step, head, rest),
            shape((requests, cols), F32),
            "vvh",
            moves(rest * 2 * step * cols, rest * flops // 2),
            40,
            [VMEM((min(15, rest), step, cols), BF16), dma((min(15, rest),))],
        )(rows, acc, in_hbm(up_weight))

    other = swap(base(False))
    mine = base(True)
    return call(final_kernel, shape((requests, cols), BF16), "vvvv")(
        sel, mine, other, received.reshape(batches * OWN_MOST, cols)
    )


def solution(mesh):
    in_specs = (
        P(("group", "batch"), "tensor"),
        P("tensor", "batch"),
        P(("group", "batch"), "tensor", None),
        P(("group", "batch"), "tensor", None),
        P("group"),
        P("group"),
    )
    return jax.shard_map(
        per_device,
        mesh=mesh,
        in_specs=in_specs,
        out_specs=P("group", ("batch", "tensor")),
        check_vma=False,
    )
```

```python
import functools

import jax
import jax.numpy as jnp
from jax import lax
from jax.experimental import pallas as pl
from jax.experimental.pallas import tpu as pltpu
from jax.sharding import PartitionSpec as P

OWN_MOST = 8
LANES = 128
MIB = 1 << 20
F32 = jnp.float32
BF16 = jnp.bfloat16
VMEM = pltpu.VMEM


def whole(n):
    return [pl.BlockSpec(memory_space=VMEM)] * n


def in_vmem(x):
    return pltpu.with_memory_space_constraint(x, VMEM)


def in_hbm(x):
    return pltpu.with_memory_space_constraint(x, pltpu.HBM)


def order_of(batches):
    return sorted(range(batches), key=lambda b: abs(2 * b - batches + 1))


def place_in_order(b, batches):
    return jnp.where(2 * b < batches, batches - 2 - 2 * b, 2 * b - batches + 1)


def exchange(x):
    batches = lax.axis_size("batch")
    return lax.all_to_all(
        x, "batch", 0, 0, tiled=True, axis_index_groups=[order_of(batches)]
    )


def ready_kernel(
    batches, ra_in, sr_in, down_ref, up_ref, upo_ref, w_ref,
    keep_ref, place_ref, sel_ref, downv_ref, upv_ref, wv_ref, ra_ref, sr_ref, stage, sems, index_sems
):
    me = lax.axis_index("batch")
    core = lax.axis_index("tensor")
    rows, hidden = up_ref.shape
    cols = hidden // (2 * batches)
    last = [
        pltpu.make_async_copy(down_ref, downv_ref, sems.at[0]),
        pltpu.make_async_copy(w_ref.at[: wv_ref.shape[0]], wv_ref, sems.at[2 * batches + 1]),
    ]
    copies = []
    for d, b in enumerate(order_of(batches)):
        span = pl.ds(pl.multiple_of((2 * b + core) * cols, LANES), cols)
        for k, ref in enumerate((up_ref, upo_ref)):
            copies.append(
                pltpu.make_async_copy(
                    ref.at[:, span],
                    stage.at[k * rows : (k + 1) * rows, d * cols : (d + 1) * cols],
                    sems.at[1 + 2 * d + k],
                )
            )
    indices = [
        pltpu.make_async_copy(ra_in, ra_ref, index_sems.at[0]),
        pltpu.make_async_copy(sr_in, sr_ref, index_sems.at[1]),
    ]
    for c in indices + copies + last:
        c.start()
    for c in indices:
        c.wait()
    requests, adapters = ra_ref.shape[1], sr_ref.shape[1]
    here = adapters // batches

    def iota(shape, dim):
        return lax.broadcasted_iota(jnp.int32, shape, dim)

    square = (requests, requests)
    ra = jnp.sum(jnp.where(iota(square, 0) == iota(square, 1), ra_ref[...], 0), axis=1, keepdims=True)
    slot = jnp.sum(
        jnp.where(iota((requests, adapters), 1) == ra, sr_ref[...], 0), axis=1, keepdims=True
    )
    first = iota((requests, batches), 1) * here
    hit = (slot >= first) & (slot < first + here)
    earlier = jnp.where(iota(square, 1) < iota(square, 0), 1.0, 0.0).astype(BF16)
    marks = jnp.where(hit, 1.0, 0.0)
    counts = jnp.dot(earlier, marks.astype(BF16), preferred_element_type=F32)
    rank = jnp.sum(counts * marks, axis=1, keepdims=True).astype(jnp.int32)
    owner = jnp.sum(jnp.where(hit, iota((requests, batches), 1), 0), axis=1, keepdims=True)
    wide = keep_ref.shape[1]
    width = wide // here
    low = (slot - me * here) * width
    column = iota((requests, wide), 1)
    keep_ref[...] = jnp.where((column >= low) & (column < low + width), 1.0, 0.0)
    mine = (owner == me) & (iota((requests, OWN_MOST), 1) == rank)
    place_ref[...] = jnp.where(mine, 1.0, 0.0).astype(BF16)
    sel_ref[...] = jnp.where(
        iota(sel_ref.shape, 1) == place_in_order(owner, batches) * OWN_MOST + rank, 1.0, 0.0
    ).astype(BF16)
    for c in copies:
        c.wait()
    back = pltpu.make_async_copy(stage, upv_ref, sems.at[2 * batches + 2])
    back.start()
    for c in last + [back]:
        c.wait()


def shrink_kernel(g_ref, down_ref, x_ref, f_ref, rows_ref):
    batches, each, _ = g_ref.shape
    for k, b in enumerate(order_of(batches)):
        rows_ref[b * each : (b + 1) * each] = g_ref[k].astype(F32)
    f_ref[...] = rows_ref[...].astype(BF16)
    x_ref[...] = lax.dot_general(
        f_ref[...], down_ref[...], (((1,), (1,)), ((), ())), preferred_element_type=F32
    )


def delta_kernel(here, x_ref, xo_ref, keep_ref, place_ref, up_ref, acc_ref, out_ref, d_ref, sems):
    batches, _, cols = d_ref.shape
    core = lax.axis_index("tensor")
    wide = x_ref.shape[1]
    rank = wide // here
    half = rank // 2
    shrunk = (x_ref[...] + xo_ref[...]).astype(BF16)
    kept = (shrunk.astype(F32) * keep_ref[...]).astype(BF16)
    rows = lax.dot_general(
        place_ref[...], kept, (((0,), (0,)), ((), ())), preferred_element_type=F32
    ).astype(BF16)
    i = lax.broadcasted_iota(jnp.int32, (wide, wide), 0)
    j = lax.broadcasted_iota(jnp.int32, (wide, wide), 1)
    side = jnp.where(j < wide // 2, core, 1 - core)
    k = jnp.where(j < wide // 2, j, j - wide // 2)
    source = jnp.zeros_like(k)
    for h in range(here):
        within = (k >= h * half) & (k < (h + 1) * half)
        source = jnp.where(within, h * rank + k - h * half, source)
    pick = jnp.where(i == source + side * half, 1.0, 0.0).astype(BF16)
    rows = jnp.dot(rows, pick, preferred_element_type=F32).astype(BF16)
    copies = []
    for d in range(batches):
        d_ref[d] = jnp.dot(
            rows, up_ref[:, d * cols : (d + 1) * cols], preferred_element_type=F32
        ).astype(BF16)
        copies.append(pltpu.make_async_copy(d_ref.at[d], out_ref.at[d], sems.at[d]))
        copies[d].start()
    for c in copies:
        c.wait()


def head_kernel(f_ref, w_ref, acc_ref):
    acc_ref[...] = jnp.dot(
        f_ref[:, : w_ref.shape[0]], w_ref[...], preferred_element_type=F32
    )


def base_kernel(
    step, first, count, f_ref, head_ref, w_ref, send_ref, mine_ref, rest_ref, send_buf, mine_buf, sems
):
    core = lax.axis_index("tensor")
    cols = send_ref.shape[1]
    other = pl.ds(pl.multiple_of((1 - core) * cols, LANES), cols)
    own = pl.ds(pl.multiple_of(core * cols, LANES), cols)
    done = mine_buf.shape[0]
    copies = []
    for i in range(count):
        rows = slice((first + i) * step, (first + i + 1) * step)
        target = mine_buf.at[i] if i < done else rest_ref.at[i - done]
        copies.append(
            (
                pltpu.make_async_copy(w_ref.at[rows, other], send_buf.at[i], sems.at[i, 0]),
                pltpu.make_async_copy(w_ref.at[rows, own], target, sems.at[i, 1]),
            )
        )
    for pair in copies:
        for c in pair:
            c.start()
    for i, (to_send, to_keep) in enumerate(copies):
        f = f_ref[:, (first + i) * step : (first + i + 1) * step]
        to_send.wait()
        part = jnp.dot(f, send_buf[i], preferred_element_type=F32)
        send_ref[...] = part + (send_ref[...] if i else head_ref[:, other])
        to_keep.wait()
        if i < done:
            part = jnp.dot(f, mine_buf[i], preferred_element_type=F32)
            mine_ref[...] = part + (mine_ref[...] if i else head_ref[:, own])


def rest_kernel(first, f_ref, mine_ref, w_ref, o_ref):
    count, step, _ = w_ref.shape
    total = mine_ref[...]
    for i in range(count):
        k = (first + i) * step
        total += jnp.dot(f_ref[:, k : k + step], w_ref[i], preferred_element_type=F32)
    o_ref[...] = total


def final_kernel(sel_ref, keep_ref, got_ref, d_ref, o_ref):
    total = keep_ref[...] + got_ref[...]
    total += jnp.dot(sel_ref[...], d_ref[...], preferred_element_type=F32)
    o_ref[...] = jnp.square(jnp.maximum(total, 0.0)).astype(BF16)


def call(kernel, out, places, cost=None, limit=6, scratch=(), outs=None):
    spec = {"v": pl.BlockSpec(memory_space=VMEM), "h": pl.BlockSpec(memory_space=pltpu.HBM),
            "a": pl.BlockSpec(memory_space=pl.ANY)}
    many = isinstance(out, (list, tuple))
    return pl.pallas_call(
        kernel,
        out_shape=out,
        in_specs=[spec[p] for p in places],
        out_specs=[spec[p] for p in outs or "v" * len(out)] if many else spec["v"],
        compiler_params=pltpu.CompilerParams(vmem_limit_bytes=limit * MIB),
        cost_estimate=cost,
        scratch_shapes=scratch,
    )


def moves(size, flops=0):
    return pl.CostEstimate(flops=flops, bytes_accessed=size, transcendentals=0)


def per_device(features, up_weight, down, up, request_adapter, storage_row):
    batches = lax.axis_size("batch")
    here, width, rank = down.shape
    hidden = up.shape[2]
    requests = request_adapter.shape[0]
    cols = up_weight.shape[1] // 2
    wide = here * rank
    shape = jax.ShapeDtypeStruct
    dma = pltpu.SemaphoreType.DMA
    swap = functools.partial(lax.ppermute, axis_name="tensor", perm=[(0, 1), (1, 0)])
    up = up.reshape(-1, hidden)
    up_other = swap(up)
    down = jnp.transpose(down, (0, 2, 1)).reshape(wide, width)
    sent = jnp.broadcast_to(features[None], (batches,) + features.shape)
    gathered = exchange(sent)
    step = 256
    head = 1
    keep, place, sel, down, up, first = call(
        functools.partial(ready_kernel, batches),
        [
            shape((requests, wide), F32),
            shape((requests, OWN_MOST), BF16),
            shape((requests, batches * OWN_MOST), BF16),
            VMEM(down.shape, BF16),
            pltpu.HBM((wide, hidden // 2), BF16),
            VMEM((head * step, 2 * cols), BF16),
        ],
        "hhhhhh",
        moves(6 * up.size),
        scratch=[
            VMEM((1, requests), jnp.int32),
            VMEM((1, storage_row.shape[0]), jnp.int32),
            VMEM((wide, hidden // 2), BF16),
            dma((3 + 2 * batches,)),
            dma((2,)),
        ],
        outs="vvvvhv",
    )(
        in_hbm(request_adapter.reshape(1, -1)),
        in_hbm(storage_row.reshape(1, -1)),
        in_hbm(down),
        in_hbm(up),
        in_hbm(up_other),
        in_hbm(up_weight),
    )
    x, rows = call(
        shrink_kernel,
        [shape((requests, wide), F32), shape((requests, width), BF16)],
        "vv",
        scratch=[VMEM((requests, width), F32)],
    )(gathered, in_vmem(down))
    x_other = swap(x)
    blocks = width // step
    flops = 2 * requests * step * 2 * cols
    acc = call(
        head_kernel,
        shape((requests, 2 * cols), F32),
        "vv",
        moves(head * 4 * step * cols, head * flops),
    )(rows, in_vmem(first))
    (delta,) = call(
        functools.partial(delta_kernel, here),
        [pltpu.HBM((batches, OWN_MOST, cols), BF16)],
        "vvvvva",
        scratch=[VMEM((batches, OWN_MOST, cols), BF16), dma((batches,))],
        outs="h",
    )(x, x_other, keep, place, up, acc)
    received = exchange(delta)
    count = blocks - head
    later = count // 2 + 1
    half = shape((requests, cols), F32)
    send, mine, rest = call(
        functools.partial(base_kernel, step, head, count),
        [half, half, VMEM((later, step, cols), BF16)],
        "vvh",
        moves(count * 4 * step * cols, count * flops),
        32,
        [
            VMEM((count, step, cols), BF16),
            VMEM((count - later, step, cols), BF16),
            dma((count, 2)),
        ],
    )(rows, acc, in_hbm(up_weight))
    other = swap(send)
    mine = call(
        functools.partial(rest_kernel, blocks - later),
        half,
        "vvv",
        moves(later * 4 * step * cols, later * flops),
    )(rows, mine, in_vmem(rest))
    return call(final_kernel, shape((requests, cols), BF16), "vvvv")(
        sel, mine, other, received.reshape(batches * OWN_MOST, cols)
    )


def solution(mesh):
    in_specs = (
        P(("group", "batch"), "tensor"),
        P("tensor", "batch"),
        P(("group", "batch"), "tensor", None),
        P(("group", "batch"), "tensor", None),
        P("group"),
        P("group"),
    )
    return jax.shard_map(
        per_device,
        mesh=mesh,
        in_specs=in_specs,
        out_specs=P("group", ("batch", "tensor")),
        check_vma=False,
    )
```

```python
import functools

import jax
import jax.numpy as jnp
from jax import lax
from jax.experimental import pallas as pl
from jax.experimental.pallas import tpu as pltpu
from jax.sharding import PartitionSpec as P

OWN_MOST = 8
LANES = 128
MIB = 1 << 20
F32 = jnp.float32
BF16 = jnp.bfloat16
VMEM = pltpu.VMEM


def whole(n):
    return [pl.BlockSpec(memory_space=VMEM)] * n


def in_vmem(x):
    return pltpu.with_memory_space_constraint(x, VMEM)


def in_hbm(x):
    return pltpu.with_memory_space_constraint(x, pltpu.HBM)


def order_of(batches):
    quarter = batches // 4
    middle = range(quarter, batches - quarter)
    return [*reversed(middle), *reversed(range(batches - quarter, batches)), *range(quarter)]


def place_in_order(b, batches):
    quarter = batches // 4
    upper = batches - quarter
    ends = jnp.where(b < quarter, upper + b, 2 * upper - 1 - b)
    return jnp.where((b >= quarter) & (b < upper), upper - 1 - b, ends)


def exchange(x):
    batches = lax.axis_size("batch")
    return lax.all_to_all(
        x, "batch", 0, 0, tiled=True, axis_index_groups=[order_of(batches)]
    )


def ready_kernel(
    batches, ra_in, sr_in, down_ref, up_ref, upo_ref, w_ref,
    keep_ref, place_ref, sel_ref, downv_ref, upv_ref, wv_ref, ra_ref, sr_ref, stage, sems, index_sems
):
    me = lax.axis_index("batch")
    core = lax.axis_index("tensor")
    rows, hidden = up_ref.shape
    cols = hidden // (2 * batches)
    last = [
        pltpu.make_async_copy(down_ref, downv_ref, sems.at[0]),
        pltpu.make_async_copy(w_ref.at[: wv_ref.shape[0]], wv_ref, sems.at[2 * batches + 1]),
    ]
    copies = []
    for d, b in enumerate(order_of(batches)):
        span = pl.ds(pl.multiple_of((2 * b + core) * cols, LANES), cols)
        for k, ref in enumerate((up_ref, upo_ref)):
            copies.append(
                pltpu.make_async_copy(
                    ref.at[:, span],
                    stage.at[k * rows : (k + 1) * rows, d * cols : (d + 1) * cols],
                    sems.at[1 + 2 * d + k],
                )
            )
    indices = [
        pltpu.make_async_copy(ra_in, ra_ref, index_sems.at[0]),
        pltpu.make_async_copy(sr_in, sr_ref, index_sems.at[1]),
    ]
    for c in indices + copies + last:
        c.start()
    for c in indices:
        c.wait()
    requests, adapters = ra_ref.shape[1], sr_ref.shape[1]
    here = adapters // batches

    def iota(shape, dim):
        return lax.broadcasted_iota(jnp.int32, shape, dim)

    square = (requests, requests)
    ra = jnp.sum(jnp.where(iota(square, 0) == iota(square, 1), ra_ref[...], 0), axis=1, keepdims=True)
    slot = jnp.sum(
        jnp.where(iota((requests, adapters), 1) == ra, sr_ref[...], 0), axis=1, keepdims=True
    )
    first = iota((requests, batches), 1) * here
    hit = (slot >= first) & (slot < first + here)
    earlier = jnp.where(iota(square, 1) < iota(square, 0), 1.0, 0.0).astype(BF16)
    marks = jnp.where(hit, 1.0, 0.0)
    counts = jnp.dot(earlier, marks.astype(BF16), preferred_element_type=F32)
    rank = jnp.sum(counts * marks, axis=1, keepdims=True).astype(jnp.int32)
    owner = jnp.sum(jnp.where(hit, iota((requests, batches), 1), 0), axis=1, keepdims=True)
    wide = keep_ref.shape[1]
    width = wide // here
    low = (slot - me * here) * width
    column = iota((requests, wide), 1)
    keep_ref[...] = jnp.where((column >= low) & (column < low + width), 1.0, 0.0)
    mine = (owner == me) & (iota((requests, OWN_MOST), 1) == rank)
    place_ref[...] = jnp.where(mine, 1.0, 0.0).astype(BF16)
    sel_ref[...] = jnp.where(
        iota(sel_ref.shape, 1) == place_in_order(owner, batches) * OWN_MOST + rank, 1.0, 0.0
    ).astype(BF16)
    for c in copies:
        c.wait()
    back = pltpu.make_async_copy(stage, upv_ref, sems.at[2 * batches + 2])
    back.start()
    for c in last + [back]:
        c.wait()


def shrink_kernel(g_ref, down_ref, x_ref, f_ref, rows_ref):
    batches, each, _ = g_ref.shape
    for k, b in enumerate(order_of(batches)):
        rows_ref[b * each : (b + 1) * each] = g_ref[k].astype(F32)
    f_ref[...] = rows_ref[...].astype(BF16)
    x_ref[...] = lax.dot_general(
        f_ref[...], down_ref[...], (((1,), (1,)), ((), ())), preferred_element_type=F32
    )


def delta_kernel(here, x_ref, xo_ref, keep_ref, place_ref, up_ref, acc_ref, out_ref, d_ref, sems):
    batches, _, cols = d_ref.shape
    core = lax.axis_index("tensor")
    wide = x_ref.shape[1]
    rank = wide // here
    half = rank // 2
    shrunk = (x_ref[...] + xo_ref[...]).astype(BF16)
    kept = (shrunk.astype(F32) * keep_ref[...]).astype(BF16)
    rows = lax.dot_general(
        place_ref[...], kept, (((0,), (0,)), ((), ())), preferred_element_type=F32
    ).astype(BF16)
    i = lax.broadcasted_iota(jnp.int32, (wide, wide), 0)
    j = lax.broadcasted_iota(jnp.int32, (wide, wide), 1)
    side = jnp.where(j < wide // 2, core, 1 - core)
    k = jnp.where(j < wide // 2, j, j - wide // 2)
    source = jnp.zeros_like(k)
    for h in range(here):
        within = (k >= h * half) & (k < (h + 1) * half)
        source = jnp.where(within, h * rank + k - h * half, source)
    pick = jnp.where(i == source + side * half, 1.0, 0.0).astype(BF16)
    rows = jnp.dot(rows, pick, preferred_element_type=F32).astype(BF16)
    copies = []
    for d in range(batches):
        d_ref[d] = jnp.dot(
            rows, up_ref[:, d * cols : (d + 1) * cols], preferred_element_type=F32
        ).astype(BF16)
        copies.append(pltpu.make_async_copy(d_ref.at[d], out_ref.at[d], sems.at[d]))
        copies[d].start()
    for c in copies:
        c.wait()


def head_kernel(f_ref, w_ref, acc_ref):
    acc_ref[...] = jnp.dot(
        f_ref[:, : w_ref.shape[0]], w_ref[...], preferred_element_type=F32
    )


def base_kernel(
    step, first, count, f_ref, head_ref, w_ref, send_ref, mine_ref, rest_ref, send_buf, mine_buf, sems
):
    core = lax.axis_index("tensor")
    cols = send_ref.shape[1]
    other = pl.ds(pl.multiple_of((1 - core) * cols, LANES), cols)
    own = pl.ds(pl.multiple_of(core * cols, LANES), cols)
    done = mine_buf.shape[0]
    copies = []
    for i in range(count):
        rows = slice((first + i) * step, (first + i + 1) * step)
        target = mine_buf.at[i] if i < done else rest_ref.at[i - done]
        copies.append(
            (
                pltpu.make_async_copy(w_ref.at[rows, other], send_buf.at[i], sems.at[i, 0]),
                pltpu.make_async_copy(w_ref.at[rows, own], target, sems.at[i, 1]),
            )
        )
    for pair in copies:
        for c in pair:
            c.start()
    for i, (to_send, to_keep) in enumerate(copies):
        f = f_ref[:, (first + i) * step : (first + i + 1) * step]
        to_send.wait()
        part = jnp.dot(f, send_buf[i], preferred_element_type=F32)
        send_ref[...] = part + (send_ref[...] if i else head_ref[:, other])
        to_keep.wait()
        if i < done:
            part = jnp.dot(f, mine_buf[i], preferred_element_type=F32)
            mine_ref[...] = part + (mine_ref[...] if i else head_ref[:, own])


def rest_kernel(first, f_ref, mine_ref, w_ref, o_ref):
    count, step, _ = w_ref.shape
    total = mine_ref[...]
    for i in range(count):
        k = (first + i) * step
        total += jnp.dot(f_ref[:, k : k + step], w_ref[i], preferred_element_type=F32)
    o_ref[...] = total


def final_kernel(sel_ref, keep_ref, got_ref, d_ref, o_ref):
    total = keep_ref[...] + got_ref[...]
    total += jnp.dot(sel_ref[...], d_ref[...], preferred_element_type=F32)
    o_ref[...] = jnp.square(jnp.maximum(total, 0.0)).astype(BF16)


def call(kernel, out, places, cost=None, limit=6, scratch=(), outs=None):
    spec = {"v": pl.BlockSpec(memory_space=VMEM), "h": pl.BlockSpec(memory_space=pltpu.HBM),
            "a": pl.BlockSpec(memory_space=pl.ANY)}
    many = isinstance(out, (list, tuple))
    return pl.pallas_call(
        kernel,
        out_shape=out,
        in_specs=[spec[p] for p in places],
        out_specs=[spec[p] for p in outs or "v" * len(out)] if many else spec["v"],
        compiler_params=pltpu.CompilerParams(vmem_limit_bytes=limit * MIB),
        cost_estimate=cost,
        scratch_shapes=scratch,
    )


def moves(size, flops=0):
    return pl.CostEstimate(flops=flops, bytes_accessed=size, transcendentals=0)


def per_device(features, up_weight, down, up, request_adapter, storage_row):
    batches = lax.axis_size("batch")
    here, width, rank = down.shape
    hidden = up.shape[2]
    requests = request_adapter.shape[0]
    cols = up_weight.shape[1] // 2
    wide = here * rank
    shape = jax.ShapeDtypeStruct
    dma = pltpu.SemaphoreType.DMA
    swap = functools.partial(lax.ppermute, axis_name="tensor", perm=[(0, 1), (1, 0)])
    up = up.reshape(-1, hidden)
    up_other = swap(up)
    down = jnp.transpose(down, (0, 2, 1)).reshape(wide, width)
    sent = jnp.broadcast_to(features[None], (batches,) + features.shape)
    gathered = exchange(sent)
    step = 256
    head = 1
    keep, place, sel, down, up, first = call(
        functools.partial(ready_kernel, batches),
        [
            shape((requests, wide), F32),
            shape((requests, OWN_MOST), BF16),
            shape((requests, batches * OWN_MOST), BF16),
            VMEM(down.shape, BF16),
            pltpu.HBM((wide, hidden // 2), BF16),
            VMEM((head * step, 2 * cols), BF16),
        ],
        "hhhhhh",
        moves(6 * up.size),
        scratch=[
            VMEM((1, requests), jnp.int32),
            VMEM((1, storage_row.shape[0]), jnp.int32),
            VMEM((wide, hidden // 2), BF16),
            dma((3 + 2 * batches,)),
            dma((2,)),
        ],
        outs="vvvvhv",
    )(
        in_hbm(request_adapter.reshape(1, -1)),
        in_hbm(storage_row.reshape(1, -1)),
        in_hbm(down),
        in_hbm(up),
        in_hbm(up_other),
        in_hbm(up_weight),
    )
    x, rows = call(
        shrink_kernel,
        [shape((requests, wide), F32), shape((requests, width), BF16)],
        "vv",
        scratch=[VMEM((requests, width), F32)],
    )(gathered, in_vmem(down))
    x_other = swap(x)
    blocks = width // step
    flops = 2 * requests * step * 2 * cols
    acc = call(
        head_kernel,
        shape((requests, 2 * cols), F32),
        "vv",
        moves(head * 4 * step * cols, head * flops),
    )(rows, in_vmem(first))
    (delta,) = call(
        functools.partial(delta_kernel, here),
        [pltpu.HBM((batches, OWN_MOST, cols), BF16)],
        "vvvvva",
        scratch=[VMEM((batches, OWN_MOST, cols), BF16), dma((batches,))],
        outs="h",
    )(x, x_other, keep, place, up, acc)
    received = exchange(delta)
    count = blocks - head
    later = count // 2 + 1
    half = shape((requests, cols), F32)
    send, mine, rest = call(
        functools.partial(base_kernel, step, head, count),
        [half, half, VMEM((later, step, cols), BF16)],
        "vvh",
        moves(count * 4 * step * cols, count * flops),
        32,
        [
            VMEM((count, step, cols), BF16),
            VMEM((count - later, step, cols), BF16),
            dma((count, 2)),
        ],
    )(rows, acc, in_hbm(up_weight))
    other = swap(send)
    mine = call(
        functools.partial(rest_kernel, blocks - later),
        half,
        "vvv",
        moves(later * 4 * step * cols, later * flops),
    )(rows, mine, in_vmem(rest))
    return call(final_kernel, shape((requests, cols), BF16), "vvvv")(
        sel, mine, other, received.reshape(batches * OWN_MOST, cols)
    )


def solution(mesh):
    in_specs = (
        P(("group", "batch"), "tensor"),
        P("tensor", "batch"),
        P(("group", "batch"), "tensor", None),
        P(("group", "batch"), "tensor", None),
        P("group"),
        P("group"),
    )
    return jax.shard_map(
        per_device,
        mesh=mesh,
        in_specs=in_specs,
        out_specs=P("group", ("batch", "tensor")),
        check_vma=False,
    )
```

```python
import functools

import jax
import jax.numpy as jnp
from jax import lax
from jax.experimental import pallas as pl
from jax.experimental.pallas import tpu as pltpu
from jax.sharding import PartitionSpec as P

OWN_MOST = 8
LANES = 128
MIB = 1 << 20
F32 = jnp.float32
BF16 = jnp.bfloat16
VMEM = pltpu.VMEM


def whole(n):
    return [pl.BlockSpec(memory_space=VMEM)] * n


def in_vmem(x):
    return pltpu.with_memory_space_constraint(x, VMEM)


def in_hbm(x):
    return pltpu.with_memory_space_constraint(x, pltpu.HBM)


def order_of(batches):
    first, quarter = batches // 2 - 1, batches // 4
    middle = [b for b in range(quarter, batches - quarter) if b != first]
    return [first, *reversed(middle), *reversed(range(batches - quarter, batches)), *range(quarter)]


def ready_kernel(
    batches, ra_in, sr_in, down_ref, up_ref, upo_ref, w_ref,
    keep_ref, place_ref, sel_ref, downv_ref, upv_ref, wv_ref, ra_ref, sr_ref, stage, sems, index_sems
):
    me = lax.axis_index("batch")
    core = lax.axis_index("tensor")
    rows, hidden = up_ref.shape
    cols = hidden // (2 * batches)
    last = [
        pltpu.make_async_copy(down_ref, downv_ref, sems.at[0]),
        pltpu.make_async_copy(w_ref.at[: wv_ref.shape[0]], wv_ref, sems.at[2 * batches + 1]),
    ]
    copies = []
    for d in range(batches):
        span = pl.ds(pl.multiple_of((2 * d + core) * cols, LANES), cols)
        for k, ref in enumerate((up_ref, upo_ref)):
            copies.append(
                pltpu.make_async_copy(
                    ref.at[:, span],
                    stage.at[k * rows : (k + 1) * rows, d * cols : (d + 1) * cols],
                    sems.at[1 + 2 * d + k],
                )
            )
    indices = [
        pltpu.make_async_copy(ra_in, ra_ref, index_sems.at[0]),
        pltpu.make_async_copy(sr_in, sr_ref, index_sems.at[1]),
    ]
    for c in indices + copies + last:
        c.start()
    for c in indices:
        c.wait()
    requests, adapters = ra_ref.shape[1], sr_ref.shape[1]
    here = adapters // batches

    def iota(shape, dim):
        return lax.broadcasted_iota(jnp.int32, shape, dim)

    square = (requests, requests)
    ra = jnp.sum(jnp.where(iota(square, 0) == iota(square, 1), ra_ref[...], 0), axis=1, keepdims=True)
    slot = jnp.sum(
        jnp.where(iota((requests, adapters), 1) == ra, sr_ref[...], 0), axis=1, keepdims=True
    )
    first = iota((requests, batches), 1) * here
    hit = (slot >= first) & (slot < first + here)
    earlier = jnp.where(iota(square, 1) < iota(square, 0), 1.0, 0.0).astype(BF16)
    marks = jnp.where(hit, 1.0, 0.0)
    counts = jnp.dot(earlier, marks.astype(BF16), preferred_element_type=F32)
    rank = jnp.sum(counts * marks, axis=1, keepdims=True).astype(jnp.int32)
    owner = jnp.sum(jnp.where(hit, iota((requests, batches), 1), 0), axis=1, keepdims=True)
    wide = keep_ref.shape[1]
    width = wide // here
    low = (slot - me * here) * width
    column = iota((requests, wide), 1)
    keep_ref[...] = jnp.where((column >= low) & (column < low + width), 1.0, 0.0)
    mine = (owner == me) & (iota((requests, OWN_MOST), 1) == rank)
    place_ref[...] = jnp.where(mine, 1.0, 0.0).astype(BF16)
    sel_ref[...] = jnp.where(
        iota(sel_ref.shape, 1) == owner * OWN_MOST + rank, 1.0, 0.0
    ).astype(BF16)
    for c in copies:
        c.wait()
    back = pltpu.make_async_copy(stage, upv_ref, sems.at[2 * batches + 2])
    back.start()
    for c in last + [back]:
        c.wait()


def shrink_kernel(g_ref, down_ref, x_ref, f_ref, rows_ref):
    batches, each, _ = g_ref.shape
    for k, b in enumerate(order_of(batches)):
        rows_ref[b * each : (b + 1) * each] = g_ref[k].astype(F32)
    f_ref[...] = rows_ref[...].astype(BF16)
    x_ref[...] = lax.dot_general(
        f_ref[...], down_ref[...], (((1,), (1,)), ((), ())), preferred_element_type=F32
    )


def delta_kernel(here, x_ref, xo_ref, keep_ref, place_ref, up_ref, acc_ref, out_ref, d_ref, sems):
    batches, _, cols = d_ref.shape
    core = lax.axis_index("tensor")
    wide = x_ref.shape[1]
    rank = wide // here
    half = rank // 2
    shrunk = (x_ref[...] + xo_ref[...]).astype(BF16)
    kept = (shrunk.astype(F32) * keep_ref[...]).astype(BF16)
    rows = lax.dot_general(
        place_ref[...], kept, (((0,), (0,)), ((), ())), preferred_element_type=F32
    ).astype(BF16)
    i = lax.broadcasted_iota(jnp.int32, (wide, wide), 0)
    j = lax.broadcasted_iota(jnp.int32, (wide, wide), 1)
    side = jnp.where(j < wide // 2, core, 1 - core)
    k = jnp.where(j < wide // 2, j, j - wide // 2)
    source = jnp.zeros_like(k)
    for h in range(here):
        within = (k >= h * half) & (k < (h + 1) * half)
        source = jnp.where(within, h * rank + k - h * half, source)
    pick = jnp.where(i == source + side * half, 1.0, 0.0).astype(BF16)
    rows = jnp.dot(rows, pick, preferred_element_type=F32).astype(BF16)
    copies = []
    for d in range(batches):
        d_ref[d] = jnp.dot(
            rows, up_ref[:, d * cols : (d + 1) * cols], preferred_element_type=F32
        ).astype(BF16)
        copies.append(pltpu.make_async_copy(d_ref.at[d], out_ref.at[d], sems.at[d]))
        copies[d].start()
    for c in copies:
        c.wait()


def head_kernel(f_ref, w_ref, acc_ref):
    acc_ref[...] = jnp.dot(
        f_ref[:, : w_ref.shape[0]], w_ref[...], preferred_element_type=F32
    )


def base_kernel(
    step, first, count, f_ref, head_ref, w_ref, send_ref, mine_ref, rest_ref, send_buf, mine_buf, sems
):
    core = lax.axis_index("tensor")
    cols = send_ref.shape[1]
    other = pl.ds(pl.multiple_of((1 - core) * cols, LANES), cols)
    own = pl.ds(pl.multiple_of(core * cols, LANES), cols)
    done = mine_buf.shape[0]
    copies = []
    for i in range(count):
        rows = slice((first + i) * step, (first + i + 1) * step)
        target = mine_buf.at[i] if i < done else rest_ref.at[i - done]
        copies.append(
            (
                pltpu.make_async_copy(w_ref.at[rows, other], send_buf.at[i], sems.at[i, 0]),
                pltpu.make_async_copy(w_ref.at[rows, own], target, sems.at[i, 1]),
            )
        )
    for pair in copies:
        for c in pair:
            c.start()
    for i, (to_send, to_keep) in enumerate(copies):
        f = f_ref[:, (first + i) * step : (first + i + 1) * step]
        to_send.wait()
        part = jnp.dot(f, send_buf[i], preferred_element_type=F32)
        send_ref[...] = part + (send_ref[...] if i else head_ref[:, other])
        to_keep.wait()
        if i < done:
            part = jnp.dot(f, mine_buf[i], preferred_element_type=F32)
            mine_ref[...] = part + (mine_ref[...] if i else head_ref[:, own])


def rest_kernel(first, f_ref, mine_ref, w_ref, o_ref):
    count, step, _ = w_ref.shape
    total = mine_ref[...]
    for i in range(count):
        k = (first + i) * step
        total += jnp.dot(f_ref[:, k : k + step], w_ref[i], preferred_element_type=F32)
    o_ref[...] = total


def final_kernel(sel_ref, keep_ref, got_ref, d_ref, o_ref):
    total = keep_ref[...] + got_ref[...]
    total += jnp.dot(sel_ref[...], d_ref[...], preferred_element_type=F32)
    o_ref[...] = jnp.square(jnp.maximum(total, 0.0)).astype(BF16)


def call(kernel, out, places, cost=None, limit=6, scratch=(), outs=None):
    spec = {"v": pl.BlockSpec(memory_space=VMEM), "h": pl.BlockSpec(memory_space=pltpu.HBM),
            "a": pl.BlockSpec(memory_space=pl.ANY)}
    many = isinstance(out, (list, tuple))
    return pl.pallas_call(
        kernel,
        out_shape=out,
        in_specs=[spec[p] for p in places],
        out_specs=[spec[p] for p in outs or "v" * len(out)] if many else spec["v"],
        compiler_params=pltpu.CompilerParams(vmem_limit_bytes=limit * MIB),
        cost_estimate=cost,
        scratch_shapes=scratch,
    )


def moves(size, flops=0):
    return pl.CostEstimate(flops=flops, bytes_accessed=size, transcendentals=0)


def per_device(features, up_weight, down, up, request_adapter, storage_row):
    batches = lax.axis_size("batch")
    here, width, rank = down.shape
    hidden = up.shape[2]
    requests = request_adapter.shape[0]
    cols = up_weight.shape[1] // 2
    wide = here * rank
    shape = jax.ShapeDtypeStruct
    dma = pltpu.SemaphoreType.DMA
    swap = functools.partial(lax.ppermute, axis_name="tensor", perm=[(0, 1), (1, 0)])
    up = up.reshape(-1, hidden)
    up_other = swap(up)
    down = jnp.transpose(down, (0, 2, 1)).reshape(wide, width)
    sent = jnp.broadcast_to(features[None], (batches,) + features.shape)
    gathered = lax.all_to_all(
        sent, "batch", 0, 0, tiled=True, axis_index_groups=[order_of(batches)]
    )
    step = 256
    head = 1
    keep, place, sel, down, up, first = call(
        functools.partial(ready_kernel, batches),
        [
            shape((requests, wide), F32),
            shape((requests, OWN_MOST), BF16),
            shape((requests, batches * OWN_MOST), BF16),
            VMEM(down.shape, BF16),
            pltpu.HBM((wide, hidden // 2), BF16),
            VMEM((head * step, 2 * cols), BF16),
        ],
        "hhhhhh",
        moves(6 * up.size),
        scratch=[
            VMEM((1, requests), jnp.int32),
            VMEM((1, storage_row.shape[0]), jnp.int32),
            VMEM((wide, hidden // 2), BF16),
            dma((3 + 2 * batches,)),
            dma((2,)),
        ],
        outs="vvvvhv",
    )(
        in_hbm(request_adapter.reshape(1, -1)),
        in_hbm(storage_row.reshape(1, -1)),
        in_hbm(down),
        in_hbm(up),
        in_hbm(up_other),
        in_hbm(up_weight),
    )
    x, rows = call(
        shrink_kernel,
        [shape((requests, wide), F32), shape((requests, width), BF16)],
        "vv",
        scratch=[VMEM((requests, width), F32)],
    )(gathered, in_vmem(down))
    x_other = swap(x)
    blocks = width // step
    flops = 2 * requests * step * 2 * cols
    acc = call(
        head_kernel,
        shape((requests, 2 * cols), F32),
        "vv",
        moves(head * 4 * step * cols, head * flops),
    )(rows, in_vmem(first))
    (delta,) = call(
        functools.partial(delta_kernel, here),
        [pltpu.HBM((batches, OWN_MOST, cols), BF16)],
        "vvvvva",
        scratch=[VMEM((batches, OWN_MOST, cols), BF16), dma((batches,))],
        outs="h",
    )(x, x_other, keep, place, up, acc)
    received = lax.all_to_all(delta, "batch", 0, 0, tiled=True)
    count = blocks - head
    later = count // 2 + 1
    half = shape((requests, cols), F32)
    send, mine, rest = call(
        functools.partial(base_kernel, step, head, count),
        [half, half, VMEM((later, step, cols), BF16)],
        "vvh",
        moves(count * 4 * step * cols, count * flops),
        32,
        [
            VMEM((count, step, cols), BF16),
            VMEM((count - later, step, cols), BF16),
            dma((count, 2)),
        ],
    )(rows, acc, in_hbm(up_weight))
    other = swap(send)
    mine = call(
        functools.partial(rest_kernel, blocks - later),
        half,
        "vvv",
        moves(later * 4 * step * cols, later * flops),
    )(rows, mine, in_vmem(rest))
    return call(final_kernel, shape((requests, cols), BF16), "vvvv")(
        sel, mine, other, received.reshape(batches * OWN_MOST, cols)
    )


def solution(mesh):
    in_specs = (
        P(("group", "batch"), "tensor"),
        P("tensor", "batch"),
        P(("group", "batch"), "tensor", None),
        P(("group", "batch"), "tensor", None),
        P("group"),
        P("group"),
    )
    return jax.shard_map(
        per_device,
        mesh=mesh,
        in_specs=in_specs,
        out_specs=P("group", ("batch", "tensor")),
        check_vma=False,
    )
```

```python
import functools

import jax
import jax.numpy as jnp
from jax import lax
from jax.experimental import pallas as pl
from jax.experimental.pallas import tpu as pltpu
from jax.sharding import PartitionSpec as P

OWN_MOST = 8
LANES = 128
MIB = 1 << 20
F32 = jnp.float32
BF16 = jnp.bfloat16
VMEM = pltpu.VMEM


def whole(n):
    return [pl.BlockSpec(memory_space=VMEM)] * n


def in_vmem(x):
    return pltpu.with_memory_space_constraint(x, VMEM)


def in_hbm(x):
    return pltpu.with_memory_space_constraint(x, pltpu.HBM)


def order_of(batches):
    first, quarter = batches // 2 - 1, batches // 4
    middle = [b for b in range(quarter, batches - quarter) if b != first]
    return [first, *reversed(middle), *reversed(range(batches - quarter, batches)), *range(quarter)]


def ready_kernel(
    batches, ra_in, sr_in, down_ref, up_ref, upo_ref, w_ref,
    keep_ref, place_ref, sel_ref, downv_ref, upv_ref, wv_ref, ra_ref, sr_ref, stage, down_buf, sems, index_sems
):
    me = lax.axis_index("batch")
    core = lax.axis_index("tensor")
    rows, hidden = up_ref.shape
    cols = hidden // (2 * batches)
    last = [
        pltpu.make_async_copy(down_ref, down_buf, sems.at[0]),
        pltpu.make_async_copy(w_ref.at[: wv_ref.shape[0]], wv_ref, sems.at[2 * batches + 1]),
    ]
    copies = []
    for d in range(batches):
        span = pl.ds(pl.multiple_of((2 * d + core) * cols, LANES), cols)
        for k, ref in enumerate((up_ref, upo_ref)):
            copies.append(
                pltpu.make_async_copy(
                    ref.at[:, span],
                    stage.at[
                        pl.ds(pl.multiple_of((core if k == 0 else 1 - core) * rows, 16), rows),
                        d * cols : (d + 1) * cols,
                    ],
                    sems.at[1 + 2 * d + k],
                )
            )
    indices = [
        pltpu.make_async_copy(ra_in, ra_ref, index_sems.at[0]),
        pltpu.make_async_copy(sr_in, sr_ref, index_sems.at[1]),
    ]
    for c in indices + copies + last:
        c.start()
    for c in indices:
        c.wait()
    requests, adapters = ra_ref.shape[1], sr_ref.shape[1]
    here = adapters // batches

    def iota(shape, dim):
        return lax.broadcasted_iota(jnp.int32, shape, dim)

    square = (requests, requests)
    ra = jnp.sum(jnp.where(iota(square, 0) == iota(square, 1), ra_ref[...], 0), axis=1, keepdims=True)
    slot = jnp.sum(
        jnp.where(iota((requests, adapters), 1) == ra, sr_ref[...], 0), axis=1, keepdims=True
    )
    first = iota((requests, batches), 1) * here
    hit = (slot >= first) & (slot < first + here)
    earlier = jnp.where(iota(square, 1) < iota(square, 0), 1.0, 0.0).astype(BF16)
    marks = jnp.where(hit, 1.0, 0.0)
    counts = jnp.dot(earlier, marks.astype(BF16), preferred_element_type=F32)
    rank = jnp.sum(counts * marks, axis=1, keepdims=True).astype(jnp.int32)
    owner = jnp.sum(jnp.where(hit, iota((requests, batches), 1), 0), axis=1, keepdims=True)
    wide = keep_ref.shape[1]
    half = wide // here // 2
    column = iota((requests, wide), 1)
    within = jnp.where(column < wide // 2, column, column - wide // 2)
    low = (slot - me * here) * half
    keep_ref[...] = jnp.where((within >= low) & (within < low + half), 1.0, 0.0)
    mine = (owner == me) & (iota((requests, OWN_MOST), 1) == rank)
    place_ref[...] = jnp.where(mine, 1.0, 0.0).astype(BF16)
    sel_ref[...] = jnp.where(
        iota(sel_ref.shape, 1) == owner * OWN_MOST + rank, 1.0, 0.0
    ).astype(BF16)
    for c in copies:
        c.wait()
    back = pltpu.make_async_copy(stage, upv_ref, sems.at[2 * batches + 2])
    back.start()
    last[0].wait()
    row, column = iota((wide, wide), 0), iota((wide, wide), 1)
    source = jnp.zeros_like(row)
    for h in range(here):
        for k in range(2):
            start = (k * here + h) * half
            inside = (row >= start) & (row < start + half)
            source = jnp.where(inside, (2 * h + k) * half + row - start, source)
    pick = jnp.where(column == source, 1.0, 0.0).astype(BF16)
    downv_ref[...] = jnp.dot(pick, down_buf[...], preferred_element_type=F32).astype(BF16)
    for c in [last[1], back]:
        c.wait()


def shrink_kernel(g_ref, down_ref, x_ref, f_ref, rows_ref):
    batches, each, _ = g_ref.shape
    for k, b in enumerate(order_of(batches)):
        rows_ref[b * each : (b + 1) * each] = g_ref[k].astype(F32)
    f_ref[...] = rows_ref[...].astype(BF16)
    x_ref[...] = lax.dot_general(
        f_ref[...], down_ref[...], (((1,), (1,)), ((), ())), preferred_element_type=F32
    )


def delta_kernel(x_ref, xo_ref, keep_ref, place_ref, up_ref, acc_ref, out_ref, d_ref, sems):
    batches, _, cols = d_ref.shape
    shrunk = (x_ref[...] + xo_ref[...]).astype(BF16)
    kept = (shrunk.astype(F32) * keep_ref[...]).astype(BF16)
    rows = lax.dot_general(
        place_ref[...], kept, (((0,), (0,)), ((), ())), preferred_element_type=F32
    ).astype(BF16)
    copies = []
    for d in range(batches):
        d_ref[d] = jnp.dot(
            rows, up_ref[:, d * cols : (d + 1) * cols], preferred_element_type=F32
        ).astype(BF16)
        copies.append(pltpu.make_async_copy(d_ref.at[d], out_ref.at[d], sems.at[d]))
        copies[d].start()
    for c in copies:
        c.wait()


def head_kernel(f_ref, w_ref, acc_ref):
    acc_ref[...] = jnp.dot(
        f_ref[:, : w_ref.shape[0]], w_ref[...], preferred_element_type=F32
    )


def base_kernel(
    step, first, count, f_ref, head_ref, w_ref, send_ref, mine_ref, rest_ref, send_buf, mine_buf, sems
):
    core = lax.axis_index("tensor")
    cols = send_ref.shape[1]
    other = pl.ds(pl.multiple_of((1 - core) * cols, LANES), cols)
    own = pl.ds(pl.multiple_of(core * cols, LANES), cols)
    done = mine_buf.shape[0]
    copies = []
    for i in range(count):
        rows = slice((first + i) * step, (first + i + 1) * step)
        target = mine_buf.at[i] if i < done else rest_ref.at[i - done]
        copies.append(
            (
                pltpu.make_async_copy(w_ref.at[rows, other], send_buf.at[i], sems.at[i, 0]),
                pltpu.make_async_copy(w_ref.at[rows, own], target, sems.at[i, 1]),
            )
        )
    for pair in copies:
        for c in pair:
            c.start()
    for i, (to_send, to_keep) in enumerate(copies):
        f = f_ref[:, (first + i) * step : (first + i + 1) * step]
        to_send.wait()
        part = jnp.dot(f, send_buf[i], preferred_element_type=F32)
        send_ref[...] = part + (send_ref[...] if i else head_ref[:, other])
        to_keep.wait()
        if i < done:
            part = jnp.dot(f, mine_buf[i], preferred_element_type=F32)
            mine_ref[...] = part + (mine_ref[...] if i else head_ref[:, own])


def rest_kernel(first, f_ref, mine_ref, w_ref, o_ref):
    count, step, _ = w_ref.shape
    total = mine_ref[...]
    for i in range(count):
        k = (first + i) * step
        total += jnp.dot(f_ref[:, k : k + step], w_ref[i], preferred_element_type=F32)
    o_ref[...] = total


def final_kernel(sel_ref, keep_ref, got_ref, d_ref, o_ref):
    total = keep_ref[...] + got_ref[...]
    total += jnp.dot(sel_ref[...], d_ref[...], preferred_element_type=F32)
    o_ref[...] = jnp.square(jnp.maximum(total, 0.0)).astype(BF16)


def call(kernel, out, places, cost=None, limit=6, scratch=(), outs=None):
    spec = {"v": pl.BlockSpec(memory_space=VMEM), "h": pl.BlockSpec(memory_space=pltpu.HBM),
            "a": pl.BlockSpec(memory_space=pl.ANY)}
    many = isinstance(out, (list, tuple))
    return pl.pallas_call(
        kernel,
        out_shape=out,
        in_specs=[spec[p] for p in places],
        out_specs=[spec[p] for p in outs or "v" * len(out)] if many else spec["v"],
        compiler_params=pltpu.CompilerParams(vmem_limit_bytes=limit * MIB),
        cost_estimate=cost,
        scratch_shapes=scratch,
    )


def moves(size, flops=0):
    return pl.CostEstimate(flops=flops, bytes_accessed=size, transcendentals=0)


def per_device(features, up_weight, down, up, request_adapter, storage_row):
    batches = lax.axis_size("batch")
    here, width, rank = down.shape
    hidden = up.shape[2]
    requests = request_adapter.shape[0]
    cols = up_weight.shape[1] // 2
    wide = here * rank
    shape = jax.ShapeDtypeStruct
    dma = pltpu.SemaphoreType.DMA
    swap = functools.partial(lax.ppermute, axis_name="tensor", perm=[(0, 1), (1, 0)])
    up = up.reshape(-1, hidden)
    up_other = swap(up)
    down = jnp.transpose(down, (0, 2, 1)).reshape(wide, width)
    sent = jnp.broadcast_to(features[None], (batches,) + features.shape)
    gathered = lax.all_to_all(
        sent, "batch", 0, 0, tiled=True, axis_index_groups=[order_of(batches)]
    )
    step = 256
    head = 1
    keep, place, sel, down, up, first = call(
        functools.partial(ready_kernel, batches),
        [
            shape((requests, wide), F32),
            shape((requests, OWN_MOST), BF16),
            shape((requests, batches * OWN_MOST), BF16),
            VMEM(down.shape, BF16),
            pltpu.HBM((wide, hidden // 2), BF16),
            VMEM((head * step, 2 * cols), BF16),
        ],
        "hhhhhh",
        moves(6 * up.size),
        scratch=[
            VMEM((1, requests), jnp.int32),
            VMEM((1, storage_row.shape[0]), jnp.int32),
            VMEM((wide, hidden // 2), BF16),
            VMEM(down.shape, BF16),
            dma((3 + 2 * batches,)),
            dma((2,)),
        ],
        outs="vvvvhv",
    )(
        in_hbm(request_adapter.reshape(1, -1)),
        in_hbm(storage_row.reshape(1, -1)),
        in_hbm(down),
        in_hbm(up),
        in_hbm(up_other),
        in_hbm(up_weight),
    )
    x, rows = call(
        shrink_kernel,
        [shape((requests, wide), F32), shape((requests, width), BF16)],
        "vv",
        scratch=[VMEM((requests, width), F32)],
    )(gathered, in_vmem(down))
    x_other = swap(x)
    blocks = width // step
    flops = 2 * requests * step * 2 * cols
    acc = call(
        head_kernel,
        shape((requests, 2 * cols), F32),
        "vv",
        moves(head * 4 * step * cols, head * flops),
    )(rows, in_vmem(first))
    (delta,) = call(
        delta_kernel,
        [pltpu.HBM((batches, OWN_MOST, cols), BF16)],
        "vvvvva",
        scratch=[VMEM((batches, OWN_MOST, cols), BF16), dma((batches,))],
        outs="h",
    )(x, x_other, keep, place, up, acc)
    received = lax.all_to_all(delta, "batch", 0, 0, tiled=True)
    count = blocks - head
    later = count // 2 + 1
    half = shape((requests, cols), F32)
    send, mine, rest = call(
        functools.partial(base_kernel, step, head, count),
        [half, half, VMEM((later, step, cols), BF16)],
        "vvh",
        moves(count * 4 * step * cols, count * flops),
        32,
        [
            VMEM((count, step, cols), BF16),
            VMEM((count - later, step, cols), BF16),
            dma((count, 2)),
        ],
    )(rows, acc, in_hbm(up_weight))
    other = swap(send)
    mine = call(
        functools.partial(rest_kernel, blocks - later),
        half,
        "vvv",
        moves(later * 4 * step * cols, later * flops),
    )(rows, mine, in_vmem(rest))
    return call(final_kernel, shape((requests, cols), BF16), "vvvv")(
        sel, mine, other, received.reshape(batches * OWN_MOST, cols)
    )


def solution(mesh):
    in_specs = (
        P(("group", "batch"), "tensor"),
        P("tensor", "batch"),
        P(("group", "batch"), "tensor", None),
        P(("group", "batch"), "tensor", None),
        P("group"),
        P("group"),
    )
    return jax.shard_map(
        per_device,
        mesh=mesh,
        in_specs=in_specs,
        out_specs=P("group", ("batch", "tensor")),
        check_vma=False,
    )
```

```python
import functools

import jax
import jax.numpy as jnp
from jax import lax
from jax.experimental import pallas as pl
from jax.experimental.pallas import tpu as pltpu
from jax.sharding import PartitionSpec as P

OWN_MOST = 8
LANES = 128
MIB = 1 << 20
F32 = jnp.float32
BF16 = jnp.bfloat16
VMEM = pltpu.VMEM


def whole(n):
    return [pl.BlockSpec(memory_space=VMEM)] * n


def in_vmem(x):
    return pltpu.with_memory_space_constraint(x, VMEM)


def in_hbm(x):
    return pltpu.with_memory_space_constraint(x, pltpu.HBM)


def order_of(batches):
    first, quarter = batches // 2 - 1, batches // 4
    middle = [b for b in range(quarter, batches - quarter) if b != first]
    return [first, *reversed(middle), *reversed(range(batches - quarter, batches)), *range(quarter)]


def ready_kernel(
    batches, ra_in, sr_in, down_ref, up_ref, upo_ref, w_ref,
    keep_ref, place_ref, sel_ref, downv_ref, upv_ref, wv_ref, ra_ref, sr_ref, stage, down_buf, sems, index_sems
):
    me = lax.axis_index("batch")
    core = lax.axis_index("tensor")
    rows, hidden = up_ref.shape
    cols = hidden // (2 * batches)
    last = [
        pltpu.make_async_copy(down_ref, down_buf, sems.at[0]),
        pltpu.make_async_copy(w_ref.at[: wv_ref.shape[0]], wv_ref, sems.at[2 * batches + 1]),
    ]
    copies = []
    for d in range(batches):
        span = pl.ds(pl.multiple_of((2 * d + core) * cols, LANES), cols)
        for k, ref in enumerate((up_ref, upo_ref)):
            copies.append(
                pltpu.make_async_copy(
                    ref.at[:, span],
                    stage.at[
                        pl.ds(pl.multiple_of((core if k == 0 else 1 - core) * rows, 16), rows),
                        d * cols : (d + 1) * cols,
                    ],
                    sems.at[1 + 2 * d + k],
                )
            )
    indices = [
        pltpu.make_async_copy(ra_in, ra_ref, index_sems.at[0]),
        pltpu.make_async_copy(sr_in, sr_ref, index_sems.at[1]),
    ]
    for c in indices + copies + last:
        c.start()
    for c in indices:
        c.wait()
    requests, adapters = ra_ref.shape[1], sr_ref.shape[1]
    here = adapters // batches

    def iota(shape, dim):
        return lax.broadcasted_iota(jnp.int32, shape, dim)

    square = (requests, requests)
    ra = jnp.sum(jnp.where(iota(square, 0) == iota(square, 1), ra_ref[...], 0), axis=1, keepdims=True)
    slot = jnp.sum(
        jnp.where(iota((requests, adapters), 1) == ra, sr_ref[...], 0), axis=1, keepdims=True
    )
    first = iota((requests, batches), 1) * here
    hit = (slot >= first) & (slot < first + here)
    earlier = jnp.where(iota(square, 1) < iota(square, 0), 1.0, 0.0).astype(BF16)
    marks = jnp.where(hit, 1.0, 0.0)
    counts = jnp.dot(earlier, marks.astype(BF16), preferred_element_type=F32)
    rank = jnp.sum(counts * marks, axis=1, keepdims=True).astype(jnp.int32)
    owner = jnp.sum(jnp.where(hit, iota((requests, batches), 1), 0), axis=1, keepdims=True)
    wide = keep_ref.shape[1]
    half = wide // here // 2
    column = iota((requests, wide), 1)
    within = jnp.where(column < wide // 2, column, column - wide // 2)
    low = (slot - me * here) * half
    keep_ref[...] = jnp.where((within >= low) & (within < low + half), 1.0, 0.0)
    mine = (owner == me) & (iota((requests, OWN_MOST), 1) == rank)
    place_ref[...] = jnp.where(mine, 1.0, 0.0).astype(BF16)
    sel_ref[...] = jnp.where(
        iota(sel_ref.shape, 1) == owner * OWN_MOST + rank, 1.0, 0.0
    ).astype(BF16)
    for c in copies:
        c.wait()
    back = pltpu.make_async_copy(stage, upv_ref, sems.at[2 * batches + 2])
    back.start()
    last[0].wait()
    row, column = iota((wide, wide), 0), iota((wide, wide), 1)
    source = jnp.zeros_like(row)
    for h in range(here):
        for k in range(2):
            start = (k * here + h) * half
            inside = (row >= start) & (row < start + half)
            source = jnp.where(inside, (2 * h + k) * half + row - start, source)
    pick = jnp.where(column == source, 1.0, 0.0).astype(BF16)
    downv_ref[...] = jnp.dot(pick, down_buf[...], preferred_element_type=F32).astype(BF16)
    for c in [last[1], back]:
        c.wait()


def shrink_kernel(g_ref, down_ref, x_ref, f_ref, rows_ref):
    batches, each, _ = g_ref.shape
    for k, b in enumerate(order_of(batches)):
        rows_ref[b * each : (b + 1) * each] = g_ref[k].astype(F32)
    f_ref[...] = rows_ref[...].astype(BF16)
    x_ref[...] = lax.dot_general(
        f_ref[...], down_ref[...], (((1,), (1,)), ((), ())), preferred_element_type=F32
    )


def delta_kernel(x_ref, xo_ref, keep_ref, place_ref, up_ref, acc_ref, d_ref):
    batches, _, cols = d_ref.shape
    shrunk = (x_ref[...] + xo_ref[...]).astype(BF16)
    kept = (shrunk.astype(F32) * keep_ref[...]).astype(BF16)
    rows = lax.dot_general(
        place_ref[...], kept, (((0,), (0,)), ((), ())), preferred_element_type=F32
    ).astype(BF16)
    for d in range(batches):
        d_ref[d] = jnp.dot(
            rows, up_ref[:, d * cols : (d + 1) * cols], preferred_element_type=F32
        ).astype(BF16)


def head_kernel(f_ref, w_ref, acc_ref):
    acc_ref[...] = jnp.dot(
        f_ref[:, : w_ref.shape[0]], w_ref[...], preferred_element_type=F32
    )


def base_kernel(
    step, first, count, f_ref, head_ref, w_ref, send_ref, mine_ref, rest_ref, send_buf, mine_buf, sems
):
    core = lax.axis_index("tensor")
    cols = send_ref.shape[1]
    other = pl.ds(pl.multiple_of((1 - core) * cols, LANES), cols)
    own = pl.ds(pl.multiple_of(core * cols, LANES), cols)
    done = mine_buf.shape[0]
    copies = []
    for i in range(count):
        rows = slice((first + i) * step, (first + i + 1) * step)
        target = mine_buf.at[i] if i < done else rest_ref.at[i - done]
        copies.append(
            (
                pltpu.make_async_copy(w_ref.at[rows, other], send_buf.at[i], sems.at[i, 0]),
                pltpu.make_async_copy(w_ref.at[rows, own], target, sems.at[i, 1]),
            )
        )
    for pair in copies:
        for c in pair:
            c.start()
    for i, (to_send, to_keep) in enumerate(copies):
        f = f_ref[:, (first + i) * step : (first + i + 1) * step]
        to_send.wait()
        part = jnp.dot(f, send_buf[i], preferred_element_type=F32)
        send_ref[...] = part + (send_ref[...] if i else head_ref[:, other])
        to_keep.wait()
        if i < done:
            part = jnp.dot(f, mine_buf[i], preferred_element_type=F32)
            mine_ref[...] = part + (mine_ref[...] if i else head_ref[:, own])


def rest_kernel(first, f_ref, mine_ref, w_ref, o_ref):
    count, step, _ = w_ref.shape
    total = mine_ref[...]
    for i in range(count):
        k = (first + i) * step
        total += jnp.dot(f_ref[:, k : k + step], w_ref[i], preferred_element_type=F32)
    o_ref[...] = total


def final_kernel(sel_ref, keep_ref, got_ref, d_ref, o_ref):
    total = keep_ref[...] + got_ref[...]
    total += jnp.dot(sel_ref[...], d_ref[...], preferred_element_type=F32)
    o_ref[...] = jnp.square(jnp.maximum(total, 0.0)).astype(BF16)


def call(kernel, out, places, cost=None, limit=6, scratch=(), outs=None):
    spec = {"v": pl.BlockSpec(memory_space=VMEM), "h": pl.BlockSpec(memory_space=pltpu.HBM),
            "a": pl.BlockSpec(memory_space=pl.ANY)}
    many = isinstance(out, (list, tuple))
    return pl.pallas_call(
        kernel,
        out_shape=out,
        in_specs=[spec[p] for p in places],
        out_specs=[spec[p] for p in outs or "v" * len(out)] if many else spec["v"],
        compiler_params=pltpu.CompilerParams(vmem_limit_bytes=limit * MIB),
        cost_estimate=cost,
        scratch_shapes=scratch,
    )


def moves(size, flops=0):
    return pl.CostEstimate(flops=flops, bytes_accessed=size, transcendentals=0)


def per_device(features, up_weight, down, up, request_adapter, storage_row):
    batches = lax.axis_size("batch")
    here, width, rank = down.shape
    hidden = up.shape[2]
    requests = request_adapter.shape[0]
    cols = up_weight.shape[1] // 2
    wide = here * rank
    shape = jax.ShapeDtypeStruct
    dma = pltpu.SemaphoreType.DMA
    swap = functools.partial(lax.ppermute, axis_name="tensor", perm=[(0, 1), (1, 0)])
    up = up.reshape(-1, hidden)
    up_other = swap(up)
    down = jnp.transpose(down, (0, 2, 1)).reshape(wide, width)
    sent = jnp.broadcast_to(features[None], (batches,) + features.shape)
    gathered = lax.all_to_all(
        sent, "batch", 0, 0, tiled=True, axis_index_groups=[order_of(batches)]
    )
    step = 256
    head = 1
    keep, place, sel, down, up, first = call(
        functools.partial(ready_kernel, batches),
        [
            shape((requests, wide), F32),
            shape((requests, OWN_MOST), BF16),
            shape((requests, batches * OWN_MOST), BF16),
            VMEM(down.shape, BF16),
            pltpu.HBM((wide, hidden // 2), BF16),
            VMEM((head * step, 2 * cols), BF16),
        ],
        "hhhhhh",
        moves(6 * up.size),
        scratch=[
            VMEM((1, requests), jnp.int32),
            VMEM((1, storage_row.shape[0]), jnp.int32),
            VMEM((wide, hidden // 2), BF16),
            VMEM(down.shape, BF16),
            dma((3 + 2 * batches,)),
            dma((2,)),
        ],
        outs="vvvvhv",
    )(
        in_hbm(request_adapter.reshape(1, -1)),
        in_hbm(storage_row.reshape(1, -1)),
        in_hbm(down),
        in_hbm(up),
        in_hbm(up_other),
        in_hbm(up_weight),
    )
    x, rows = call(
        shrink_kernel,
        [shape((requests, wide), F32), shape((requests, width), BF16)],
        "vv",
        scratch=[VMEM((requests, width), F32)],
    )(gathered, in_vmem(down))
    x_other = swap(x)
    blocks = width // step
    flops = 2 * requests * step * 2 * cols
    acc = call(
        head_kernel,
        shape((requests, 2 * cols), F32),
        "vv",
        moves(head * 4 * step * cols, head * flops),
    )(rows, in_vmem(first))
    (delta,) = call(
        delta_kernel,
        [pltpu.HBM((batches, OWN_MOST, cols), BF16)],
        "vvvvva",
    )(x, x_other, keep, place, up, acc)
    received = lax.all_to_all(delta, "batch", 0, 0, tiled=True)
    count = blocks - head
    later = count // 2 + 1
    half = shape((requests, cols), F32)
    send, mine, rest = call(
        functools.partial(base_kernel, step, head, count),
        [half, half, VMEM((later, step, cols), BF16)],
        "vvh",
        moves(count * 4 * step * cols, count * flops),
        32,
        [
            VMEM((count, step, cols), BF16),
            VMEM((count - later, step, cols), BF16),
            dma((count, 2)),
        ],
    )(rows, acc, in_hbm(up_weight))
    other = swap(send)
    mine = call(
        functools.partial(rest_kernel, blocks - later),
        half,
        "vvv",
        moves(later * 4 * step * cols, later * flops),
    )(rows, mine, in_vmem(rest))
    return call(final_kernel, shape((requests, cols), BF16), "vvvv")(
        sel, mine, other, received.reshape(batches * OWN_MOST, cols)
    )


def solution(mesh):
    in_specs = (
        P(("group", "batch"), "tensor"),
        P("tensor", "batch"),
        P(("group", "batch"), "tensor", None),
        P(("group", "batch"), "tensor", None),
        P("group"),
        P("group"),
    )
    return jax.shard_map(
        per_device,
        mesh=mesh,
        in_specs=in_specs,
        out_specs=P("group", ("batch", "tensor")),
        check_vma=False,
    )
```
